32 devices in a mesh: dp: 4 (over x, core), cent: 8 (over z, y).
Axes of the slice: x: 2, y: 2, z: 4, core: 2. Of those that a mesh axis runs over, the one named last changes fastest.
Arguments:
- embeddings: bfloat16 [4096, 4096], P('dp', 'cent'), may hold values from -6 to 6
- centroids: bfloat16 [4096, 4096], P('cent'), may hold values from -0.1875 to 0.1875
- assignment: int32 [4096], P('dp'), may hold values from 0 to 4095, as said below
- prior_counts: int32 [4096], P('cent'), may hold values from 1 to 4
Outputs:
- top_score: float32 [4096], P('dp')
- updated: float32 [4096, 4096], P('dp', 'cent')
The draws below stay inside these ranges and needn't reach their ends.
Inputs may be any that keep to these rules, and one draw needn't show every extreme that they name: `assignment`: cluster k belongs to index k // 512 of cent. Among the 1024 rows of one index of dp, at most 256 have clusters that belong to one index of cent, and in every such block of rows some index of cent gets exactly 256 of them.
All inputs are finite; a program needn't handle non-finite values.
Results may differ from the reference program's by a relative error of at most 0.0003.
Values may be sent and summed in bfloat16 or wider, within the bound.
No kernel may reach another device: no remote copies, remote signals or barrier semaphores. Data moves between devices by JAX's collectives and lax.ppermute only.
A program may use at most 64 MiB of HBM per device.

```python
import jax
import jax.numpy as jnp
from jax import lax

D = 4096
CENT_DEV = 512
ROWS_DEV = 1024
ROWS = 4096
CENTROIDS = 4096
CAP = 256
N_DP = 4
N_CENT = 8


def draw_assignment(key, part):
    key = jax.random.fold_in(key, 11)

    def one_block(block_key):
        key_full, key_order, key_slots, key_local = jax.random.split(block_key, 4)
        full_owner = jax.random.randint(key_full, (), 0, N_CENT, dtype=jnp.int32)
        order = jax.random.permutation(key_order, ROWS_DEV)
        slots = jax.random.permutation(key_slots, (N_CENT - 1) * CAP)[:ROWS_DEV]
        others = (slots // CAP).astype(jnp.int32)
        others = others + (others >= full_owner).astype(jnp.int32)
        owner = jnp.where(order < CAP, full_owner, others).astype(jnp.int32)
        local = jax.random.randint(key_local, (ROWS_DEV,), 0, CENT_DEV, dtype=jnp.int32)
        return owner * CENT_DEV + local
    block_keys = jax.random.split(key, N_DP)
    return jax.vmap(one_block)(block_keys).reshape(ROWS).astype(jnp.int32)


def touch_ends(values, own_key, low, largest):
    longest = values.shape.index(max(values.shape))
    spots = []
    for shift in (0, 1):
        where = [jax.random.randint(jax.random.fold_in(own_key, axis), (), 0, length) for axis, length in enumerate(values.shape)]
        where[longest] = (where[longest] + shift) % values.shape[longest]
        spots.append(tuple(where))
    return values.at[spots[0]].set(low).at[spots[1]].set(largest)


def level_of(key, dims, cuts, smallest, largest):
    gain, own = 1.0, jax.random.fold_in(key, 6)
    for position, blocks in cuts:
        draws = jnp.exp(jax.random.uniform(jax.random.fold_in(own, position), (blocks,), jnp.float32, smallest / len(cuts), largest / len(cuts)))
        gain = gain * jnp.repeat(draws, dims[position] // blocks).reshape([-1 if axis == position else 1 for axis in range(len(dims))])
    return gain


def bell_draw(rng, extent, width, most, shards=(), held_as=jnp.bfloat16):
    entries = width * jax.random.normal(rng, extent, jnp.float32)
    if shards:
        entries = entries * level_of(rng, extent, shards, -0.22, 0.18)
    return jnp.clip(entries, -most, most).astype(held_as)


def setup_inputs(seed: int = 0) -> dict:
    keys = jax.random.split(jax.random.key(seed), 5)
    return {
        "embeddings": bell_draw(keys[0], (ROWS, D), 1.0, 6.0, ((0, 4), (1, 8))),
        "centroids": bell_draw(keys[1], (CENTROIDS, D), (D // 4) ** -0.5, 0.1875, ((0, 8),)),
        "assignment": draw_assignment(jax.random.fold_in(keys[4], 71), 0),
        "prior_counts": touch_ends(jax.random.randint(keys[3], (CENTROIDS,), 1, 5), jax.random.fold_in(keys[3], 1), 1, 4).astype(jnp.int32),
    }


def reference(embeddings, centroids, assignment, prior_counts):
    cent_f = centroids.astype(jnp.float32)
    half_norm = 0.5 * jnp.sum(cent_f * cent_f, axis=1)
    block = 512
    rows_f = embeddings.astype(jnp.float32).reshape(ROWS // block, block, D) if ROWS % block == 0 else embeddings.astype(jnp.float32).reshape(1, ROWS, D)

    def best_of(rows_block):
        score = jnp.dot(rows_block, cent_f.T, preferred_element_type=jnp.float32) - half_norm[None, :]
        return jnp.max(score, axis=1)

    top_score = lax.map(best_of, rows_f).reshape(ROWS)
    sums = jax.ops.segment_sum(embeddings.astype(jnp.float32), assignment, CENTROIDS)
    counts = jax.ops.segment_sum(jnp.ones((ROWS,), jnp.float32), assignment, CENTROIDS)
    prior = prior_counts.astype(jnp.float32)
    updated = (prior[:, None] * cent_f + sums) / (prior + counts)[:, None]
    return top_score, updated.T
```

```python
import jax
import jax.numpy as jnp
from jax import lax
from jax.experimental import pallas as pl
from jax.experimental.pallas import tpu as pltpu
from jax.sharding import PartitionSpec as P

VMEM = pl.BlockSpec(memory_space=pltpu.VMEM)
SMEM = pl.BlockSpec(memory_space=pltpu.SMEM)
PARAMS = pltpu.CompilerParams(vmem_limit_bytes=16 * 1024 * 1024)

ABOVE, HERE, BELOW = 0, 1, 2


class Steps:
    def __init__(self):
        self.token = jnp.zeros((8, 128), jnp.int32)

    def tie(self, *values):
        self.token, values = lax.optimization_barrier((self.token, values))
        return values[0] if len(values) == 1 else values


def chosen_rows(shift, first, count, half):
    at = lax.broadcasted_iota(jnp.int32, (count, half), 0) + (shift + first)
    at = jnp.where(at >= half, at - half, at)
    at = jnp.where(at >= half, at - half, at)
    hit = at == lax.broadcasted_iota(jnp.int32, (count, half), 1)
    return hit.astype(jnp.float32).astype(jnp.bfloat16)


def product(hot, rows):
    return jnp.dot(hot, rows, preferred_element_type=jnp.float32)


def between(starts_ref, has, wants, half):
    start = 0 if has is None else starts_ref[has]
    return lax.rem(starts_ref[wants] - start + 2 * half, half)


def turn(parts, starts, has, wants, first, count, split):
    half = sum(p.shape[0] for p in parts) if split else parts[0].shape[0]
    width = parts[0].shape[1] if split else sum(p.shape[1] for p in parts)

    def kernel(starts_ref, *refs):
        out_ref = refs[-1]
        hot = chosen_rows(between(starts_ref, has, wants, half), first, count, half)
        if split:
            near = refs[0].shape[0]
            total = product(hot[:, :near], refs[0][...]) + product(hot[:, near:], refs[1][...])
            out_ref[...] = total.astype(jnp.bfloat16)
        else:
            low = 0
            for ref in refs[:-1]:
                high = low + ref.shape[1]
                out_ref[:, low:high] = product(hot, ref[...]).astype(jnp.bfloat16)
                low = high

    return pl.pallas_call(
        kernel,
        in_specs=[SMEM] + [VMEM] * len(parts),
        out_specs=VMEM,
        out_shape=jax.ShapeDtypeStruct((count, width), jnp.bfloat16),
        compiler_params=PARAMS,
        cost_estimate=pl.CostEstimate(
            flops=2 * count * half * width, bytes_accessed=4 * half * width, transcendentals=0
        ),
        name="turn",
    )(starts, *parts)


def turn_down(kept, swapped, starts, near):
    half, width = kept.shape

    def kernel(starts_ref, kept_ref, swapped_ref, near_ref, far_ref):
        for n, (ref, has) in enumerate(((kept_ref, ABOVE), (swapped_ref, None))):
            hot = chosen_rows(between(starts_ref, has, BELOW, half), 0, half, half)
            rows = product(hot, ref[...]).astype(jnp.bfloat16)
            near_ref[:, n * width : (n + 1) * width] = rows[:near]
            far_ref[:, n * width : (n + 1) * width] = rows[near:]

    return pl.pallas_call(
        kernel,
        in_specs=[SMEM, VMEM, VMEM],
        out_specs=[VMEM, VMEM],
        out_shape=[
            jax.ShapeDtypeStruct((near, 2 * width), jnp.bfloat16),
            jax.ShapeDtypeStruct((half - near, 2 * width), jnp.bfloat16),
        ],
        compiler_params=PARAMS,
        cost_estimate=pl.CostEstimate(
            flops=4 * half * half * width, bytes_accessed=8 * half * width, transcendentals=0
        ),
        name="turn_down",
    )(starts, kept, swapped)


def take_share(ids, table, n_dp, late):
    count, depth = table.shape[0] // n_dp // (2 if late else 1), table.shape[1]

    def kernel(ids_ref, in_ref, out_ref):
        out_ref[...] = in_ref[...]

    return pl.pallas_call(
        kernel,
        grid_spec=pltpu.PrefetchScalarGridSpec(
            num_scalar_prefetch=1,
            grid=(1,),
            in_specs=[
                pl.BlockSpec(
                    (count, depth),
                    lambda g, ids: (2 * (ids[0] ^ (n_dp // 2)) + 1 if late else ids[0], 0),
                )
            ],
            out_specs=VMEM,
        ),
        out_shape=jax.ShapeDtypeStruct((count, depth), table.dtype),
        compiler_params=PARAMS,
        cost_estimate=pl.CostEstimate(
            flops=0, bytes_accessed=4 * count * depth, transcendentals=0
        ),
        name="take_share",
    )(ids, table)


def prepare(ids, starts, clusters, orders, kept, swapped, prior, table, cap):
    half, width = kept.shape
    n_dp, rows = clusters.shape
    own, feats = table.shape[0], table.shape[1] // n_dp

    def kernel(ids_ref, starts_ref, cluster_ref, order_ref, kept_ref, swapped_ref, prior_ref,
               table_ref, self_a, self_b, same_ref, across_ref, counts_ref, base_ref):
        for out_ref, ref, has in ((self_a, kept_ref, ABOVE), (self_b, swapped_ref, None)):
            hot = chosen_rows(between(starts_ref, has, HERE, half), 0, half, half)
            out_ref[...] = product(hot, ref[...]).astype(jnp.bfloat16)
        me = ids_ref[1]
        side, place = me & 1, me >> 1
        counts = jnp.zeros((1, own), jnp.float32)
        slot = lax.broadcasted_iota(jnp.int32, (cap, rows), 0)
        column = lax.broadcasted_iota(jnp.int32, (cap, own), 1).astype(jnp.float32)
        for m in range(n_dp):
            order, cluster = order_ref[m : m + 1, :], cluster_ref[m : m + 1, :]
            local = cluster - me * own
            local = jnp.where((local >= 0) & (local < own), local, own).astype(jnp.float32)
            earlier = (cluster < (2 * place + 1) * own).astype(jnp.float32)
            before = jnp.sum(earlier, axis=1, keepdims=True).astype(jnp.int32)
            for b, out_ref in enumerate((same_ref, across_ref)):
                which = side if b == 0 else 1 - side
                start = ((before + 1 - which) >> 1) - cap + half
                turned = (order >> 1) - start + 2 * half
                turned = jnp.where(turned >= 2 * half, turned - 2 * half, turned)
                turned = jnp.where(turned >= half, turned - half, turned)
                spot = jnp.where((order & 1) == which, turned - side * cap, rows)
                name = jnp.sum(jnp.where(slot == spot, local, 0.0), axis=1, keepdims=True)
                match = (column == name).astype(jnp.float32)
                out_ref[m * cap : (m + 1) * cap, :] = match.astype(jnp.bfloat16)
                counts = counts + jnp.sum(match, axis=0, keepdims=True)
        counts_ref[...] = counts
        base_ref[...] = table_ref[...].astype(jnp.float32).T * prior_ref[...]

    outs = [
        jax.ShapeDtypeStruct((half, width), jnp.bfloat16),
        jax.ShapeDtypeStruct((half, width), jnp.bfloat16),
        jax.ShapeDtypeStruct((n_dp * cap, own), jnp.bfloat16),
        jax.ShapeDtypeStruct((n_dp * cap, own), jnp.bfloat16),
        jax.ShapeDtypeStruct((1, own), jnp.float32),
        jax.ShapeDtypeStruct((feats, own), jnp.float32),
    ]
    return pl.pallas_call(
        kernel,
        grid_spec=pltpu.PrefetchScalarGridSpec(
            num_scalar_prefetch=2,
            grid=(1,),
            in_specs=[VMEM] * 5 + [pl.BlockSpec((own, feats), lambda g, ids, at: (0, ids[0]))],
            out_specs=[VMEM] * len(outs),
        ),
        out_shape=outs,
        compiler_params=PARAMS,
        cost_estimate=pl.CostEstimate(
            flops=4 * half * half * width, bytes_accessed=16 * half * width, transcendentals=0
        ),
        name="prepare",
    )(ids, starts, clusters, orders, kept, swapped, prior, table)


def collect(ids, windows, cap, n_dp):
    n_windows, per_dp = len(windows), len(windows) // n_dp
    wide = sum(part.shape[1] for part in windows[0])
    counts = [len(window) for window in windows]
    parts = [part for window in windows for part in window]

    def kernel(ids_ref, *refs):
        part_refs, out_refs = refs[: len(parts)], refs[len(parts) :]
        side, place = ids_ref[1] & 1, ids_ref[1] >> 1
        for m in range(n_dp):
            for e in range(per_dp):
                start = 0
                wanted = lax.rem(place - (ids_ref[0] ^ m) * per_dp - e + n_windows, n_windows)
                for n, count in enumerate(counts):

                    @pl.when(wanted == n)
                    def _(m=m, e=e, start=start, count=count):
                        low = e * wide
                        for ref in part_refs[start : start + count]:
                            high = low + ref.shape[1]
                            for b in (0, 1):
                                which = side if b == 0 else 1 - side
                                rows = pl.ds(pl.multiple_of(which * cap, cap), cap)
                                out_refs[2 * m + b][:, low:high] = ref[rows, :]
                            low = high

                    start += count

    outs = [jax.ShapeDtypeStruct((cap, per_dp * wide), jnp.bfloat16)] * (2 * n_dp)
    found = pl.pallas_call(
        kernel,
        in_specs=[SMEM] + [VMEM] * len(parts),
        out_specs=[VMEM] * len(outs),
        out_shape=outs,
        compiler_params=PARAMS,
        cost_estimate=pl.CostEstimate(
            flops=0, bytes_accessed=8 * n_dp * cap * per_dp * wide, transcendentals=0
        ),
        name="collect",
    )(ids, *parts)
    return {(m, b): found[2 * m + b] for m in range(n_dp) for b in (0, 1)}


def update(ids, same_rows, across_rows, same, across, base, prior, counts, token):
    n_rows, cap = len(same_rows), same_rows[0].shape[0]
    feats, own = base.shape
    width = feats // 2

    def kernel(ids_ref, *refs):
        same_refs, across_refs = refs[:n_rows], refs[n_rows : 2 * n_rows]
        same_ref, across_ref, base_ref, prior_ref, counts_ref, token_ref, out_ref = refs[
            2 * n_rows :
        ]
        nothing = token_ref[:1, :1].astype(jnp.float32)
        inverse = 1.0 / (prior_ref[...] + counts_ref[...] + nothing)
        step = pl.program_id(0)
        for n in (0, 1):

            @pl.when(step == n)
            def _(n=n):
                total = base_ref[...]
                for row_refs, match_ref, part in (
                    (same_refs, same_ref, n),
                    (across_refs, across_ref, 1 - n),
                ):
                    held = jnp.concatenate(
                        [ref[:, part * width : (part + 1) * width] for ref in row_refs], axis=0
                    )
                    total += lax.dot_general(
                        held,
                        match_ref[...],
                        (((0,), (0,)), ((), ())),
                        preferred_element_type=jnp.float32,
                    )
                out_ref[...] = total * inverse

    block = pl.BlockSpec((width, own), lambda g, ids: (g ^ (ids[1] & 1), 0))
    return pl.pallas_call(
        kernel,
        grid_spec=pltpu.PrefetchScalarGridSpec(
            num_scalar_prefetch=1,
            grid=(2,),
            in_specs=[VMEM] * (2 * n_rows + 2) + [block, VMEM, VMEM, VMEM],
            out_specs=block,
        ),
        out_shape=jax.ShapeDtypeStruct((feats, own), jnp.float32),
        compiler_params=PARAMS,
        cost_estimate=pl.CostEstimate(
            flops=4 * n_rows * cap * feats * own, bytes_accessed=8 * feats * own, transcendentals=0
        ),
        name="update",
    )(ids, *same_rows, *across_rows, same, across, base, prior, counts, token)


def column_block(n_line, steps):
    def block(g, ids):
        side, place = ids[1] & 1, ids[1] >> 1
        step = steps[-1]
        for n, other in enumerate(steps[:-1]):
            step = jnp.where(g // 2 == n, other, step)
        return 2 * lax.rem(place - step + n_line, n_line) + (side ^ (g % 2))

    return block


def score_part(ids, tables, work, half, n_line, so_far=None):
    sizes = [table.shape[0] for table in tables]
    total, width = sum(sizes), tables[0].shape[1] // (2 * n_line)
    n_tables, n_blocks = len(tables), 2 * len(work)
    block = column_block(n_line, [step for step, _ in work])
    parts = [part for _, piece in work for part in piece]
    before = [] if so_far is None else [so_far]

    def kernel(ids_ref, *refs):
        table_refs, part_refs = refs[:n_tables], list(refs[n_tables : n_tables + len(parts)])
        before_refs = refs[n_tables + len(parts) : -5]
        out_ref, best_ref, piece, score, squares = refs[-5:]
        step = pl.program_id(0)

        @pl.when(step == 0)
        def _():
            score[...] = before_refs[0][...] if before_refs else jnp.zeros_like(score)
            squares[...] = jnp.zeros_like(squares)

        for at, (_, held) in enumerate(work):
            held_refs = [part_refs.pop(0) for _ in held]
            for n in (0, 1):

                @pl.when(step == 2 * at + n)
                def _(n=n, held_refs=held_refs):
                    if held_refs[0].shape[1] == width:
                        piece[...] = held_refs[n][...]
                    else:
                        low = 0
                        for ref in held_refs:
                            high = low + ref.shape[0]
                            piece[low:high] = ref[:, n * width : (n + 1) * width]
                            low = high
                        if low < half:
                            piece[low:] = jnp.zeros((half - low, width), piece.dtype)

        low = 0
        for ref, size in zip(table_refs, sizes):
            score[low : low + size] += lax.dot_general(
                ref[...], piece[...], (((1,), (1,)), ((), ())), preferred_element_type=jnp.float32
            )
            for lane in range(0, width, 128):
                entries = ref[:, lane : lane + 128].astype(jnp.float32)
                squares[low : low + size] += entries * entries
            low += size

        @pl.when(step == n_blocks - 1)
        def _():
            final = score[...] - 0.5 * jnp.sum(squares[...], axis=1, keepdims=True)
            out_ref[...] = final
            best_ref[...] = jnp.max(final, axis=0, keepdims=True)

    grid_spec = pltpu.PrefetchScalarGridSpec(
        num_scalar_prefetch=1,
        grid=(n_blocks,),
        in_specs=[
            pl.BlockSpec((size, width), lambda g, ids: (0, block(g, ids))) for size in sizes
        ]
        + [VMEM] * (len(parts) + len(before)),
        out_specs=[VMEM, VMEM],
        scratch_shapes=[
            pltpu.VMEM((half, width), jnp.bfloat16),
            pltpu.VMEM((total, half), jnp.float32),
            pltpu.VMEM((total, 128), jnp.float32),
        ],
    )
    return pl.pallas_call(
        kernel,
        grid_spec=grid_spec,
        out_shape=[
            jax.ShapeDtypeStruct((total, half), jnp.float32),
            jax.ShapeDtypeStruct((1, half), jnp.float32),
        ],
        compiler_params=PARAMS,
        cost_estimate=pl.CostEstimate(
            flops=2 * half * total * width * n_blocks,
            bytes_accessed=2 * total * width * n_blocks,
            transcendentals=0,
        ),
        name="score_part",
    )(ids, *tables, *parts, *before)


def score_last(ids, starts, tables, last, scores, bests, order, near, n_line):
    count, width = last.shape[0], last.shape[1] // 2
    half, rows = scores[0].shape[1], order.shape[1]
    sizes = [table.shape[0] for table in tables]
    total, n_tables, n_scores = sum(sizes), len(tables), len(scores)
    block = column_block(n_line, [n_line // 2])
    low_row = near if near % 128 == 0 else 0

    def kernel(ids_ref, starts_ref, *refs):
        table_refs, last_ref = refs[:n_tables], refs[n_tables]
        score_refs = refs[n_tables + 1 : n_tables + 1 + n_scores]
        best_refs = refs[n_tables + 1 + n_scores : n_tables + 1 + 2 * n_scores]
        order_ref, out_ref, piece, sums = refs[n_tables + 1 + 2 * n_scores :]
        step = pl.program_id(0)
        if low_row < near:
            piece[: near - low_row] = jnp.zeros((near - low_row, width), piece.dtype)
        for n in (0, 1):

            @pl.when(step == n)
            def _(n=n):
                piece[near - low_row :] = last_ref[:, n * width : (n + 1) * width]

        low = 0
        for ref, size in zip(table_refs, sizes):
            part = lax.dot_general(
                ref[...], piece[...], (((1,), (1,)), ((), ())), preferred_element_type=jnp.float32
            )
            sums[low : low + size] = part + jnp.where(step == 0, 0.0, sums[low : low + size])
            low += size

        @pl.when(step == 1)
        def _():
            late, low = [], 0
            for ref in score_refs:
                high = low + ref.shape[0]
                score = sums[low:high] + ref[:, low_row:]
                late.append(jnp.max(score, axis=0, keepdims=True))
                low = high
            row = largest_of(late)
            if low_row:
                first = largest_of([ref[:, :low_row] for ref in best_refs])
                row = jnp.concatenate([first, row], axis=1)
            column = jnp.broadcast_to(row, (8, half)).T[:, :1]
            side = ids_ref[1] & 1
            order = order_ref[...]
            turned = (order >> 1) - starts_ref[HERE] + 2 * half
            turned = jnp.where(turned >= 2 * half, turned - 2 * half, turned)
            turned = jnp.where(turned >= half, turned - half, turned)
            ours = (order & 1) == side
            found = lax.broadcasted_iota(jnp.int32, (half, rows), 0) == turned
            best = jnp.sum(jnp.where(found, column, 0.0), axis=0, keepdims=True)
            out_ref[...] = jnp.where(ours, best, -jnp.inf)

    grid_spec = pltpu.PrefetchScalarGridSpec(
        num_scalar_prefetch=2,
        grid=(2,),
        in_specs=[
            pl.BlockSpec((size, width), lambda g, ids, at: (0, block(g, ids))) for size in sizes
        ]
        + [VMEM] * (2 + 2 * n_scores),
        out_specs=VMEM,
        scratch_shapes=[
            pltpu.VMEM((half - low_row, width), jnp.bfloat16),
            pltpu.VMEM((total, half - low_row), jnp.float32),
        ],
    )
    return pl.pallas_call(
        kernel,
        grid_spec=grid_spec,
        out_shape=jax.ShapeDtypeStruct((1, rows), jnp.float32),
        compiler_params=PARAMS,
        cost_estimate=pl.CostEstimate(
            flops=4 * count * total * width, bytes_accessed=4 * total * width, transcendentals=0
        ),
        name="score_last",
    )(ids, starts, *tables, last, *scores, *bests, order)


def on_device(embeddings, centroids, assignment, prior_counts):
    n_dp, n_cent = lax.axis_size("dp"), lax.axis_size("cent")
    rows, width = embeddings.shape
    own, depth = centroids.shape
    half, n_line = rows // 2, n_cent // 2
    per_dp = n_line // n_dp
    cap = rows // n_cent
    near = 2 * cap
    middle = n_line // 2
    me_dp, me = lax.axis_index("dp"), lax.axis_index("cent")
    side, place = me % 2, me // 2
    swap = [(j, j ^ 1) for j in range(n_cent)]

    def ring(shift):
        return [(j, (j + 2 * shift) % n_cent) for j in range(n_cent)]

    def send(value, pairs):
        return lax.ppermute(value, "cent", pairs)

    ids = jnp.stack([me_dp, me])
    owner_of = assignment // own
    key = owner_of * rows + jnp.arange(rows, dtype=jnp.int32)
    order = jnp.sum(key[None, :] < key[:, None], axis=1, dtype=jnp.int32)
    parity, turn_no = order % 2, order // 2
    layers = (place + jnp.array([1, 0, n_line - 1], jnp.int32)) % n_line
    before = jnp.sum(owner_of[None, :] <= 2 * layers[:, None], axis=1, dtype=jnp.int32)
    starts = (before + 1 - side) // 2 - cap + half
    with jax.named_scope("deal_rows"):
        slot = jnp.where(parity == side, (turn_no - starts[ABOVE] + 2 * half) % half, half + turn_no)
        deal = jnp.arange(rows, dtype=jnp.int32)[:, None] == slot[None, :]
        dealt = lax.dot_general(
            deal.astype(jnp.bfloat16),
            embeddings,
            (((1,), (0,)), ((), ())),
            preferred_element_type=jnp.float32,
        ).astype(jnp.bfloat16)

    steps = Steps()
    kept, given, assignment, order, centroids, ids, starts = steps.tie(
        dealt[:half], dealt[half:], assignment, order, centroids, ids, starts
    )
    up_a, swapped = send(kept, ring(1)), send(given, swap)
    blocks = jnp.stack([assignment, order])[None]
    prior = prior_counts.astype(jnp.float32)[None, :]
    order = order[None, :]
    share = take_share(ids, centroids, n_dp, False)

    swapped, share, blocks, prior, order = steps.tie(swapped, share, blocks, prior, order)
    up_b, up_a = steps.tie(turn([swapped], starts, None, ABOVE, 0, half, False), up_a)
    up_b = send(up_b, ring(1))
    close, far, share = steps.tie(*turn_down(kept, swapped, starts, near), share)
    close, share = send(close, ring(-1)), send(share, swap)

    blocks, held_from = steps.tie(blocks), [0]
    bit = n_dp // 2
    while bit:
        pairs = [(d, d ^ bit) for d in range(n_dp)]
        blocks = jnp.concatenate([blocks, lax.ppermute(blocks, "dp", pairs)], axis=0)
        held_from = held_from + [m ^ bit for m in held_from]
        bit //= 2
        blocks = steps.tie(blocks)

    ids, centroids = steps.tie(ids, centroids)
    late_share = take_share(ids, centroids, n_dp, True)

    up_b, close, share, late_share = steps.tie(up_b, close, share, late_share)
    up = (up_a, up_b)
    pieces = {1: up}
    for step in range(2, middle):
        wide = send(turn(list(up), starts, HERE, ABOVE, 0, half, False), ring(1))
        up = (wide[:, :width], wide[:, width:])
        pieces[step] = up
    middle_near, share, late_share = steps.tie(
        turn(list(up), starts, HERE, ABOVE, 0, near, False), share, late_share
    )
    middle_near = send(middle_near, ring(1))

    others, bit = [share], n_dp // 2
    if n_dp == 4:
        pairs = [(d, d ^ bit) for d in range(n_dp)]
        others = [
            share,
            lax.ppermute(share[: share.shape[0] // 2], "dp", pairs),
            send(late_share, swap),
        ]
    else:
        while bit > 1:
            pairs = [(d, d ^ bit) for d in range(n_dp)]
            others = others + [lax.ppermute(p, "dp", pairs) for p in others]
            bit //= 2
    clusters, orders, centroids = steps.tie(blocks[:, 0], blocks[:, 1], centroids)
    self_a, self_b, same, across, counts, base = prepare(
        ids, starts, clusters, orders, kept, swapped, prior, centroids, cap
    )
    pieces[0] = (self_a, self_b)

    middle_near, pieces[0], same, across, counts, base = steps.tie(
        middle_near, pieces[0], same, across, counts, base
    )
    far = send(steps.tie(far), ring(-1))
    windows = dict(pieces)
    windows[middle], windows[n_line - 1] = (middle_near,), (close,)

    down = (close, far)
    downs = {n_line - 1: down}

    def deliver(value, m, b):
        pairs = [
            (d * n_cent + j, (d ^ m) * n_cent + (j ^ b)) for d in range(n_dp) for j in range(n_cent)
        ]
        return lax.ppermute(value, ("dp", "cent"), pairs)

    for step in range(2, middle):
        down = tuple(
            send(turn(list(down), starts, HERE, BELOW, first, count, True), ring(-1))
            for first, count in ((0, near), (near, half - near))
        )
        downs[n_line - step] = down
        windows[n_line - step] = (down[0],)
    first = [(m, 0) for m in range(2, n_dp)] + [(0, 1), (1, 1)]
    second = [(m, 1) for m in range(2, n_dp)] + [(1, 0)]
    got = steps.tie(collect(ids, [windows[n] for n in range(n_line)], cap, n_dp))
    others = steps.tie(others)
    core_sent = steps.tie(jnp.concatenate(others, axis=0))
    core = lax.ppermute(core_sent, "dp", [(d, d ^ 1) for d in range(n_dp)])
    for key in first:
        got[key] = deliver(got[key], *key)

    core, pieces = steps.tie(core, pieces)
    tables = [centroids, core_sent, core]
    work = [(step, pieces[step]) for step in pieces] + [(middle, (middle_near,))]
    so_far, _ = score_part(ids, tables, work, half, n_line)
    so_far = steps.tie(so_far)
    got.update(zip(first, steps.tie(*[got[key] for key in first])))

    downs[n_line - 1] = (close, steps.tie(downs[n_line - 1][1]))
    middle_far = steps.tie(
        turn(list(downs[middle + 1]), starts, HERE, BELOW, near, half - near, True)
    )
    middle_far = send(middle_far, ring(-1))
    for key, value in zip(second, steps.tie(*[got[key] for key in second])):
        got[key] = deliver(value, *key)
    downs = steps.tie(downs)
    work = [(step, downs[step]) for step in downs]
    score, best = steps.tie(*score_part(ids, tables, work, half, n_line, so_far))

    middle_far, got[1, 0] = steps.tie(middle_far, got[1, 0])
    best = score_last(
        ids, starts, tables, middle_far, [score], [best], order, near, n_line
    )[0]
    best = steps.tie(best)
    arrived = [send(best, ring(step)) for step in range(1, n_line)]

    got = steps.tie(got)
    feats = 2 * per_dp * width
    if per_dp == 1:
        updated = update(
            ids,
            [got[m, 0] for m in held_from],
            [got[m, 1] for m in held_from],
            same,
            across,
            base,
            prior,
            counts,
            steps.token,
        )
    else:
        counts = counts + steps.token[0, 0].astype(jnp.float32)

        def summed(match, b):
            held = jnp.concatenate([got[m, b] for m in held_from], axis=0)
            total = lax.dot_general(
                held, match, (((0,), (0,)), ((), ())), preferred_element_type=jnp.float32
            )
            return total.reshape(per_dp, 2, width, own)

        from_same, from_across = summed(same, 0), summed(across, 1)
        mine = from_same[:, 0] + from_across[:, 1]
        theirs = from_same[:, 1] + from_across[:, 0]
        even = jnp.where(side == 0, mine, theirs)
        odd = jnp.where(side == 0, theirs, mine)
        sums = jnp.stack([even, odd], axis=1).reshape(base.shape)
        updated = (base + sums) / (prior + counts)
    best, updated = steps.tie(best, updated)
    best = largest_of([best] + arrived)
    return (jnp.maximum(best, send(best, swap)), updated)


def largest_of(values):
    largest = values[0]
    for value in values[1:]:
        largest = jnp.maximum(largest, value)
    return largest


def solution(mesh):
    placed = (P("dp", "cent"), P("cent", None), P("dp"), P("cent"))
    return jax.shard_map(
        on_device, mesh=mesh, in_specs=placed, out_specs=(P("dp"), P("dp", "cent")), check_vma=False
    )
```

```python
import jax
import jax.numpy as jnp
from jax import lax
from jax.experimental import pallas as pl
from jax.experimental.pallas import tpu as pltpu
from jax.sharding import PartitionSpec as P

VMEM = pl.BlockSpec(memory_space=pltpu.VMEM)
SMEM = pl.BlockSpec(memory_space=pltpu.SMEM)
NO_COST = pl.CostEstimate(flops=0, bytes_accessed=0, transcendentals=0)
PARAMS = pltpu.CompilerParams(vmem_limit_bytes=16 * 1024 * 1024)

ABOVE, HERE, BELOW = 0, 1, 2


class Steps:
    def __init__(self):
        self.token = jnp.zeros((8, 128), jnp.int32)

    def tie(self, *values):
        self.token, values = lax.optimization_barrier((self.token, values))
        return values[0] if len(values) == 1 else values


def chosen_rows(shift, first, count, half):
    at = lax.broadcasted_iota(jnp.int32, (count, half), 0) + (shift + first)
    at = jnp.where(at >= half, at - half, at)
    at = jnp.where(at >= half, at - half, at)
    hit = at == lax.broadcasted_iota(jnp.int32, (count, half), 1)
    return hit.astype(jnp.float32).astype(jnp.bfloat16)


def product(hot, rows):
    return jnp.dot(hot, rows, preferred_element_type=jnp.float32)


def between(starts_ref, has, wants, half):
    start = 0 if has is None else starts_ref[has]
    return lax.rem(starts_ref[wants] - start + 2 * half, half)


def turn(parts, starts, has, wants, first, count, split):
    half = sum(p.shape[0] for p in parts) if split else parts[0].shape[0]
    width = parts[0].shape[1] if split else sum(p.shape[1] for p in parts)

    def kernel(starts_ref, *refs):
        out_ref = refs[-1]
        hot = chosen_rows(between(starts_ref, has, wants, half), first, count, half)
        if split:
            near = refs[0].shape[0]
            total = product(hot[:, :near], refs[0][...]) + product(hot[:, near:], refs[1][...])
            out_ref[...] = total.astype(jnp.bfloat16)
        else:
            low = 0
            for ref in refs[:-1]:
                high = low + ref.shape[1]
                out_ref[:, low:high] = product(hot, ref[...]).astype(jnp.bfloat16)
                low = high

    return pl.pallas_call(
        kernel,
        in_specs=[SMEM] + [VMEM] * len(parts),
        out_specs=VMEM,
        out_shape=jax.ShapeDtypeStruct((count, width), jnp.bfloat16),
        compiler_params=PARAMS,
        cost_estimate=NO_COST,
        name="turn",
    )(starts, *parts)


def turn_down(kept, swapped, starts, near):
    half, width = kept.shape

    def kernel(starts_ref, kept_ref, swapped_ref, near_ref, far_ref):
        for n, (ref, has) in enumerate(((kept_ref, ABOVE), (swapped_ref, None))):
            hot = chosen_rows(between(starts_ref, has, BELOW, half), 0, half, half)
            rows = product(hot, ref[...]).astype(jnp.bfloat16)
            near_ref[:, n * width : (n + 1) * width] = rows[:near]
            far_ref[:, n * width : (n + 1) * width] = rows[near:]

    return pl.pallas_call(
        kernel,
        in_specs=[SMEM, VMEM, VMEM],
        out_specs=[VMEM, VMEM],
        out_shape=[
            jax.ShapeDtypeStruct((near, 2 * width), jnp.bfloat16),
            jax.ShapeDtypeStruct((half - near, 2 * width), jnp.bfloat16),
        ],
        compiler_params=PARAMS,
        cost_estimate=NO_COST,
        name="turn_down",
    )(starts, kept, swapped)


def take_share(ids, table, n_dp, late):
    count, depth = table.shape[0] // n_dp // (2 if late else 1), table.shape[1]

    def kernel(ids_ref, in_ref, out_ref):
        out_ref[...] = in_ref[...]

    return pl.pallas_call(
        kernel,
        grid_spec=pltpu.PrefetchScalarGridSpec(
            num_scalar_prefetch=1,
            grid=(1,),
            in_specs=[
                pl.BlockSpec(
                    (count, depth),
                    lambda g, ids: (2 * (ids[0] ^ (n_dp // 2)) + 1 if late else ids[0], 0),
                )
            ],
            out_specs=VMEM,
        ),
        out_shape=jax.ShapeDtypeStruct((count, depth), table.dtype),
        compiler_params=PARAMS,
        cost_estimate=NO_COST,
        name="take_share",
    )(ids, table)


def prepare(ids, starts, clusters, orders, kept, swapped, prior, table, cap):
    half, width = kept.shape
    n_dp, rows = clusters.shape
    own, feats = table.shape[0], table.shape[1] // n_dp

    def kernel(ids_ref, starts_ref, cluster_ref, order_ref, kept_ref, swapped_ref, prior_ref,
               table_ref, self_a, self_b, same_ref, across_ref, counts_ref, base_ref):
        for out_ref, ref, has in ((self_a, kept_ref, ABOVE), (self_b, swapped_ref, None)):
            hot = chosen_rows(between(starts_ref, has, HERE, half), 0, half, half)
            out_ref[...] = product(hot, ref[...]).astype(jnp.bfloat16)
        me = ids_ref[1]
        side, place = me & 1, me >> 1
        counts = jnp.zeros((1, own), jnp.float32)
        slot = lax.broadcasted_iota(jnp.int32, (cap, rows), 0)
        column = lax.broadcasted_iota(jnp.int32, (cap, own), 1).astype(jnp.float32)
        for m in range(n_dp):
            order, cluster = order_ref[m : m + 1, :], cluster_ref[m : m + 1, :]
            local = cluster - me * own
            local = jnp.where((local >= 0) & (local < own), local, own).astype(jnp.float32)
            earlier = (cluster < (2 * place + 1) * own).astype(jnp.float32)
            before = jnp.sum(earlier, axis=1, keepdims=True).astype(jnp.int32)
            for b, out_ref in enumerate((same_ref, across_ref)):
                which = side if b == 0 else 1 - side
                start = ((before + 1 - which) >> 1) - cap + half
                turned = (order >> 1) - start + 2 * half
                turned = jnp.where(turned >= 2 * half, turned - 2 * half, turned)
                turned = jnp.where(turned >= half, turned - half, turned)
                spot = jnp.where((order & 1) == which, turned - side * cap, rows)
                name = jnp.sum(jnp.where(slot == spot, local, 0.0), axis=1, keepdims=True)
                match = (column == name).astype(jnp.float32)
                out_ref[m * cap : (m + 1) * cap, :] = match.astype(jnp.bfloat16)
                counts = counts + jnp.sum(match, axis=0, keepdims=True)
        counts_ref[...] = counts
        base_ref[...] = table_ref[...].astype(jnp.float32).T * prior_ref[...]

    outs = [
        jax.ShapeDtypeStruct((half, width), jnp.bfloat16),
        jax.ShapeDtypeStruct((half, width), jnp.bfloat16),
        jax.ShapeDtypeStruct((n_dp * cap, own), jnp.bfloat16),
        jax.ShapeDtypeStruct((n_dp * cap, own), jnp.bfloat16),
        jax.ShapeDtypeStruct((1, own), jnp.float32),
        jax.ShapeDtypeStruct((feats, own), jnp.float32),
    ]
    return pl.pallas_call(
        kernel,
        grid_spec=pltpu.PrefetchScalarGridSpec(
            num_scalar_prefetch=2,
            grid=(1,),
            in_specs=[VMEM] * 5 + [pl.BlockSpec((own, feats), lambda g, ids, at: (0, ids[0]))],
            out_specs=[VMEM] * len(outs),
        ),
        out_shape=outs,
        compiler_params=PARAMS,
        cost_estimate=NO_COST,
        name="prepare",
    )(ids, starts, clusters, orders, kept, swapped, prior, table)


def collect(ids, windows, cap, n_dp):
    n_windows, per_dp = len(windows), len(windows) // n_dp
    wide = sum(part.shape[1] for part in windows[0])
    counts = [len(window) for window in windows]
    parts = [part for window in windows for part in window]

    def kernel(ids_ref, *refs):
        part_refs, out_refs = refs[: len(parts)], refs[len(parts) :]
        side, place = ids_ref[1] & 1, ids_ref[1] >> 1
        for m in range(n_dp):
            for e in range(per_dp):
                start = 0
                wanted = lax.rem(place - (ids_ref[0] ^ m) * per_dp - e + n_windows, n_windows)
                for n, count in enumerate(counts):

                    @pl.when(wanted == n)
                    def _(m=m, e=e, start=start, count=count):
                        low = e * wide
                        for ref in part_refs[start : start + count]:
                            high = low + ref.shape[1]
                            for b in (0, 1):
                                which = side if b == 0 else 1 - side
                                rows = pl.ds(pl.multiple_of(which * cap, cap), cap)
                                out_refs[2 * m + b][:, low:high] = ref[rows, :]
                            low = high

                    start += count

    outs = [jax.ShapeDtypeStruct((cap, per_dp * wide), jnp.bfloat16)] * (2 * n_dp)
    found = pl.pallas_call(
        kernel,
        in_specs=[SMEM] + [VMEM] * len(parts),
        out_specs=[VMEM] * len(outs),
        out_shape=outs,
        compiler_params=PARAMS,
        cost_estimate=NO_COST,
        name="collect",
    )(ids, *parts)
    return {(m, b): found[2 * m + b] for m in range(n_dp) for b in (0, 1)}


def update(ids, rows, matches, base, prior, counts, token, divide):
    n_rows, cap = len(rows), rows[0][2].shape[0]
    feats, own = base.shape
    width = feats // 2

    def kernel(ids_ref, *refs):
        row_refs, match_refs = refs[:n_rows], refs[n_rows : n_rows + 2]
        base_ref, prior_ref, counts_ref, token_ref, out_ref = refs[n_rows + 2 :]
        step = pl.program_id(0)
        for n in (0, 1):

            @pl.when(step == n)
            def _(n=n):
                held, match = [], []
                for (at, b, _), ref in zip(rows, row_refs):
                    part = n ^ b
                    held.append(ref[:, part * width : (part + 1) * width])
                    match.append(match_refs[b][at * cap : (at + 1) * cap])
                total = base_ref[...] + lax.dot_general(
                    jnp.concatenate(held, axis=0),
                    jnp.concatenate(match, axis=0),
                    (((0,), (0,)), ((), ())),
                    preferred_element_type=jnp.float32,
                )
                if divide:
                    nothing = token_ref[:1, :1].astype(jnp.float32)
                    total = total * (1.0 / (prior_ref[...] + counts_ref[...] + nothing))
                out_ref[...] = total

    block = pl.BlockSpec((width, own), lambda g, ids: (g ^ (ids[1] & 1), 0))
    return pl.pallas_call(
        kernel,
        grid_spec=pltpu.PrefetchScalarGridSpec(
            num_scalar_prefetch=1,
            grid=(2,),
            in_specs=[VMEM] * (n_rows + 2) + [block, VMEM, VMEM, VMEM],
            out_specs=block,
        ),
        out_shape=jax.ShapeDtypeStruct((feats, own), jnp.float32),
        compiler_params=PARAMS,
        cost_estimate=NO_COST,
        name="update",
    )(ids, *[value for _, _, value in rows], *matches, base, prior, counts, token)


def column_block(n_line, steps):
    def block(g, ids):
        side, place = ids[1] & 1, ids[1] >> 1
        step = steps[-1]
        for n, other in enumerate(steps[:-1]):
            step = jnp.where(g // 2 == n, other, step)
        return 2 * lax.rem(place - step + n_line, n_line) + (side ^ (g % 2))

    return block


def score_part(ids, tables, work, half, n_line, so_far=None):
    sizes = [table.shape[0] for table in tables]
    total, width = sum(sizes), tables[0].shape[1] // (2 * n_line)
    n_tables, n_blocks = len(tables), 2 * len(work)
    block = column_block(n_line, [step for step, _ in work])
    parts = [part for _, piece in work for part in piece]
    before = [] if so_far is None else [so_far]

    def kernel(ids_ref, *refs):
        table_refs, part_refs = refs[:n_tables], list(refs[n_tables : n_tables + len(parts)])
        before_refs = refs[n_tables + len(parts) : -5]
        out_ref, best_ref, piece, score, squares = refs[-5:]
        step = pl.program_id(0)

        @pl.when(step == 0)
        def _():
            score[...] = before_refs[0][...] if before_refs else jnp.zeros_like(score)
            squares[...] = jnp.zeros_like(squares)

        for at, (_, held) in enumerate(work):
            held_refs = [part_refs.pop(0) for _ in held]
            for n in (0, 1):

                @pl.when(step == 2 * at + n)
                def _(n=n, held_refs=held_refs):
                    if held_refs[0].shape[1] == width:
                        piece[...] = held_refs[n][...]
                    else:
                        low = 0
                        for ref in held_refs:
                            high = low + ref.shape[0]
                            piece[low:high] = ref[:, n * width : (n + 1) * width]
                            low = high
                        if low < half:
                            piece[low:] = jnp.zeros((half - low, width), piece.dtype)

        low = 0
        for ref, size in zip(table_refs, sizes):
            score[low : low + size] += lax.dot_general(
                ref[...], piece[...], (((1,), (1,)), ((), ())), preferred_element_type=jnp.float32
            )
            for lane in range(0, width, 128):
                entries = ref[:, lane : lane + 128].astype(jnp.float32)
                squares[low : low + size] += entries * entries
            low += size

        @pl.when(step == n_blocks - 1)
        def _():
            final = score[...] - 0.5 * jnp.sum(squares[...], axis=1, keepdims=True)
            out_ref[...] = final
            best_ref[...] = jnp.max(final, axis=0, keepdims=True)

    grid_spec = pltpu.PrefetchScalarGridSpec(
        num_scalar_prefetch=1,
        grid=(n_blocks,),
        in_specs=[
            pl.BlockSpec((size, width), lambda g, ids: (0, block(g, ids))) for size in sizes
        ]
        + [VMEM] * (len(parts) + len(before)),
        out_specs=[VMEM, VMEM],
        scratch_shapes=[
            pltpu.VMEM((half, width), jnp.bfloat16),
            pltpu.VMEM((total, half), jnp.float32),
            pltpu.VMEM((total, 128), jnp.float32),
        ],
    )
    return pl.pallas_call(
        kernel,
        grid_spec=grid_spec,
        out_shape=[
            jax.ShapeDtypeStruct((total, half), jnp.float32),
            jax.ShapeDtypeStruct((1, half), jnp.float32),
        ],
        compiler_params=PARAMS,
        cost_estimate=NO_COST,
        name="score_part",
    )(ids, *tables, *parts, *before)


def score_last(ids, starts, tables, last, scores, bests, order, near, n_line):
    count, width = last.shape[0], last.shape[1] // 2
    half, rows = scores[0].shape[1], order.shape[1]
    sizes = [table.shape[0] for table in tables]
    total, n_tables, n_scores = sum(sizes), len(tables), len(scores)
    block = column_block(n_line, [n_line // 2])
    low_row = near if near % 128 == 0 else 0

    def kernel(ids_ref, starts_ref, *refs):
        table_refs, last_ref = refs[:n_tables], refs[n_tables]
        score_refs = refs[n_tables + 1 : n_tables + 1 + n_scores]
        best_refs = refs[n_tables + 1 + n_scores : n_tables + 1 + 2 * n_scores]
        order_ref, out_ref, piece, sums = refs[n_tables + 1 + 2 * n_scores :]
        step = pl.program_id(0)
        if low_row < near:
            piece[: near - low_row] = jnp.zeros((near - low_row, width), piece.dtype)
        for n in (0, 1):

            @pl.when(step == n)
            def _(n=n):
                piece[near - low_row :] = last_ref[:, n * width : (n + 1) * width]

        low = 0
        for ref, size in zip(table_refs, sizes):
            part = lax.dot_general(
                ref[...], piece[...], (((1,), (1,)), ((), ())), preferred_element_type=jnp.float32
            )
            sums[low : low + size] = part + jnp.where(step == 0, 0.0, sums[low : low + size])
            low += size

        @pl.when(step == 1)
        def _():
            late, low = [], 0
            for ref in score_refs:
                high = low + ref.shape[0]
                score = sums[low:high] + ref[:, low_row:]
                late.append(jnp.max(score, axis=0, keepdims=True))
                low = high
            row = largest_of(late)
            if low_row:
                first = largest_of([ref[:, :low_row] for ref in best_refs])
                row = jnp.concatenate([first, row], axis=1)
            column = jnp.broadcast_to(row, (8, half)).T[:, :1]
            side = ids_ref[1] & 1
            order = order_ref[...]
            turned = (order >> 1) - starts_ref[HERE] + 2 * half
            turned = jnp.where(turned >= 2 * half, turned - 2 * half, turned)
            turned = jnp.where(turned >= half, turned - half, turned)
            ours = (order & 1) == side
            found = lax.broadcasted_iota(jnp.int32, (half, rows), 0) == turned
            best = jnp.sum(jnp.where(found, column, 0.0), axis=0, keepdims=True)
            out_ref[...] = jnp.where(ours, best, -jnp.inf)

    grid_spec = pltpu.PrefetchScalarGridSpec(
        num_scalar_prefetch=2,
        grid=(2,),
        in_specs=[
            pl.BlockSpec((size, width), lambda g, ids, at: (0, block(g, ids))) for size in sizes
        ]
        + [VMEM] * (2 + 2 * n_scores),
        out_specs=VMEM,
        scratch_shapes=[
            pltpu.VMEM((half - low_row, width), jnp.bfloat16),
            pltpu.VMEM((total, half - low_row), jnp.float32),
        ],
    )
    return pl.pallas_call(
        kernel,
        grid_spec=grid_spec,
        out_shape=jax.ShapeDtypeStruct((1, rows), jnp.float32),
        compiler_params=PARAMS,
        cost_estimate=NO_COST,
        name="score_last",
    )(ids, starts, *tables, last, *scores, *bests, order)


def on_device(embeddings, centroids, assignment, prior_counts):
    n_dp, n_cent = lax.axis_size("dp"), lax.axis_size("cent")
    rows, width = embeddings.shape
    own, depth = centroids.shape
    half, n_line = rows // 2, n_cent // 2
    per_dp = n_line // n_dp
    cap = rows // n_cent
    near = 2 * cap
    middle = n_line // 2
    me_dp, me = lax.axis_index("dp"), lax.axis_index("cent")
    side, place = me % 2, me // 2
    swap = [(j, j ^ 1) for j in range(n_cent)]

    def ring(shift):
        return [(j, (j + 2 * shift) % n_cent) for j in range(n_cent)]

    def send(value, pairs):
        return lax.ppermute(value, "cent", pairs)

    ids = jnp.stack([me_dp, me])
    owner_of = assignment // own
    key = owner_of * rows + jnp.arange(rows, dtype=jnp.int32)
    order = jnp.sum(key[None, :] < key[:, None], axis=1, dtype=jnp.int32)
    parity, turn_no = order % 2, order // 2
    layers = (place + jnp.array([1, 0, n_line - 1], jnp.int32)) % n_line
    before = jnp.sum(owner_of[None, :] <= 2 * layers[:, None], axis=1, dtype=jnp.int32)
    starts = (before + 1 - side) // 2 - cap + half
    with jax.named_scope("deal_rows"):
        slot = jnp.where(parity == side, (turn_no - starts[ABOVE] + 2 * half) % half, half + turn_no)
        deal = jnp.arange(rows, dtype=jnp.int32)[:, None] == slot[None, :]
        dealt = lax.dot_general(
            deal.astype(jnp.bfloat16),
            embeddings,
            (((1,), (0,)), ((), ())),
            preferred_element_type=jnp.float32,
        ).astype(jnp.bfloat16)

    steps = Steps()
    kept, given, assignment, order, centroids, ids, starts = steps.tie(
        dealt[:half], dealt[half:], assignment, order, centroids, ids, starts
    )
    up_a, swapped = send(kept, ring(1)), send(given, swap)
    blocks = jnp.stack([assignment, order])[None]
    prior = prior_counts.astype(jnp.float32)[None, :]
    order = order[None, :]
    share = take_share(ids, centroids, n_dp, False)

    swapped, share, blocks, prior, order = steps.tie(swapped, share, blocks, prior, order)
    up_b, up_a = steps.tie(turn([swapped], starts, None, ABOVE, 0, half, False), up_a)
    up_b = send(up_b, ring(1))
    close, far = steps.tie(*turn_down(kept, swapped, starts, near))
    close, share = send(close, ring(-1)), send(steps.tie(share), swap)

    blocks, held_from = steps.tie(blocks), [0]
    bit = n_dp // 2
    while bit:
        pairs = [(d, d ^ bit) for d in range(n_dp)]
        blocks = jnp.concatenate([blocks, lax.ppermute(blocks, "dp", pairs)], axis=0)
        held_from = held_from + [m ^ bit for m in held_from]
        bit //= 2
        blocks = steps.tie(blocks)

    ids, centroids = steps.tie(ids, centroids)
    late_share = take_share(ids, centroids, n_dp, True)

    up_b, late_share = steps.tie(up_b, late_share)
    up = (up_a, up_b)
    pieces = {1: up}
    for step in range(2, middle):
        wide = send(turn(list(up), starts, HERE, ABOVE, 0, half, False), ring(1))
        up = (wide[:, :width], wide[:, width:])
        pieces[step] = up
    middle_near = steps.tie(turn(list(up), starts, HERE, ABOVE, 0, near, False))
    middle_near = send(middle_near, ring(1))
    share, late_share = steps.tie(share, late_share)

    others, bit = [share], n_dp // 2
    if n_dp == 4:
        pairs = [(d, d ^ bit) for d in range(n_dp)]
        others = [
            share,
            lax.ppermute(share[: share.shape[0] // 2], "dp", pairs),
            send(late_share, swap),
        ]
    else:
        while bit > 1:
            pairs = [(d, d ^ bit) for d in range(n_dp)]
            others = others + [lax.ppermute(p, "dp", pairs) for p in others]
            bit //= 2
    clusters, orders, centroids = steps.tie(blocks[:, 0], blocks[:, 1], centroids)
    self_a, self_b, same, across, counts, base = prepare(
        ids, starts, clusters, orders, kept, swapped, prior, centroids, cap
    )
    pieces[0] = (self_a, self_b)

    middle_near, close, pieces[0], same, across, counts, base = steps.tie(
        middle_near, close, pieces[0], same, across, counts, base
    )
    far = send(steps.tie(far), ring(-1))
    windows = dict(pieces)
    windows[middle], windows[n_line - 1] = (middle_near,), (close,)

    down = (close, far)
    downs = {n_line - 1: down}

    def deliver(value, m, b):
        pairs = [
            (d * n_cent + j, (d ^ m) * n_cent + (j ^ b)) for d in range(n_dp) for j in range(n_cent)
        ]
        return lax.ppermute(value, ("dp", "cent"), pairs)

    for step in range(2, middle):
        down = tuple(
            send(turn(list(down), starts, HERE, BELOW, first, count, True), ring(-1))
            for first, count in ((0, near), (near, half - near))
        )
        downs[n_line - step] = down
        windows[n_line - step] = (down[0],)
    first = [(2, 0), (0, 1), (1, 0)]
    second = [(m, 0) for m in range(3, n_dp)] + [(m, 1) for m in range(1, n_dp)]
    got = steps.tie(collect(ids, [windows[n] for n in range(n_line)], cap, n_dp))
    others = steps.tie(others)
    core_sent = steps.tie(jnp.concatenate(others, axis=0))
    core = lax.ppermute(core_sent, "dp", [(d, d ^ 1) for d in range(n_dp)])
    for key in first:
        got[key] = deliver(got[key], *key)

    core, pieces = steps.tie(core, pieces)
    tables = [centroids, core_sent, core]
    work = [(step, pieces[step]) for step in pieces] + [(middle, (middle_near,))]
    so_far, _ = score_part(ids, tables, work, half, n_line)
    so_far = steps.tie(so_far)
    got.update(zip(first, steps.tie(*[got[key] for key in first])))

    downs[n_line - 1] = (close, steps.tie(downs[n_line - 1][1]))
    middle_far = steps.tie(
        turn(list(downs[middle + 1]), starts, HERE, BELOW, near, half - near, True)
    )
    middle_far = send(middle_far, ring(-1))
    for key, value in zip(second, steps.tie(*[got[key] for key in second])):
        got[key] = deliver(value, *key)
    downs = steps.tie(downs)
    work = [(step, downs[step]) for step in downs]
    score, best = steps.tie(*score_part(ids, tables, work, half, n_line, so_far))

    def payloads(keys):
        return [(held_from.index(m), b, got[m, b]) for m, b in keys]

    matches = [same, across]
    if per_dp == 1:
        early = [(0, 0)] + first
        base = update(ids, payloads(early), matches, base, prior, counts, steps.token, False)
        base = steps.tie(base)

    middle_far = steps.tie(middle_far)
    best = score_last(
        ids, starts, tables, middle_far, [score], [best], order, near, n_line
    )[0]
    best = steps.tie(best)
    bit = 1
    while bit < n_line:
        pairs = [(j, j ^ (2 * bit)) for j in range(n_cent)]
        best = steps.tie(jnp.maximum(best, send(best, pairs)))
        bit *= 2
    opposite = send(best, swap)

    got = steps.tie(got)
    feats = 2 * per_dp * width
    if per_dp == 1:
        updated = update(
            ids, payloads(second), matches, base, prior, counts, steps.token, True
        )
    else:
        counts = counts + steps.token[0, 0].astype(jnp.float32)

        def summed(match, b):
            held = jnp.concatenate([got[m, b] for m in held_from], axis=0)
            total = lax.dot_general(
                held, match, (((0,), (0,)), ((), ())), preferred_element_type=jnp.float32
            )
            return total.reshape(per_dp, 2, width, own)

        from_same, from_across = summed(same, 0), summed(across, 1)
        mine = from_same[:, 0] + from_across[:, 1]
        theirs = from_same[:, 1] + from_across[:, 0]
        even = jnp.where(side == 0, mine, theirs)
        odd = jnp.where(side == 0, theirs, mine)
        sums = jnp.stack([even, odd], axis=1).reshape(base.shape)
        updated = (base + sums) / (prior + counts)
    return (jnp.maximum(best, opposite), updated)


def largest_of(values):
    largest = values[0]
    for value in values[1:]:
        largest = jnp.maximum(largest, value)
    return largest


def solution(mesh):
    placed = (P("dp", "cent"), P("cent", None), P("dp"), P("cent"))
    return jax.shard_map(
        on_device, mesh=mesh, in_specs=placed, out_specs=(P("dp"), P("dp", "cent")), check_vma=False
    )
```

```python
import jax
import jax.numpy as jnp
from jax import lax
from jax.experimental import pallas as pl
from jax.experimental.pallas import tpu as pltpu
from jax.sharding import PartitionSpec as P

VMEM = pl.BlockSpec(memory_space=pltpu.VMEM)
SMEM = pl.BlockSpec(memory_space=pltpu.SMEM)
NO_COST = pl.CostEstimate(flops=0, bytes_accessed=0, transcendentals=0)
PARAMS = pltpu.CompilerParams(vmem_limit_bytes=16 * 1024 * 1024)

ABOVE, HERE, BELOW = 0, 1, 2


class Steps:
    def __init__(self):
        self.token = jnp.zeros((8, 128), jnp.int32)

    def tie(self, *values):
        self.token, values = lax.optimization_barrier((self.token, values))
        return values[0] if len(values) == 1 else values


def chosen_rows(shift, first, count, half):
    at = lax.broadcasted_iota(jnp.int32, (count, half), 0) + (shift + first)
    at = jnp.where(at >= half, at - half, at)
    at = jnp.where(at >= half, at - half, at)
    hit = at == lax.broadcasted_iota(jnp.int32, (count, half), 1)
    return hit.astype(jnp.float32).astype(jnp.bfloat16)


def product(hot, rows):
    return jnp.dot(hot, rows, preferred_element_type=jnp.float32)


def deal(ids, clusters, embeddings, own, cap, n_line):
    rows, width = embeddings.shape
    half, chunk = rows // 2, 256
    assert own & (own - 1) == 0 and half % chunk == 0
    spread = float(-(-rows // own))

    def kernel(ids_ref, cluster_ref, rows_ref, kept_ref, given_ref, order_ref, starts_ref):
        side, place = ids_ref[1] & 1, ids_ref[1] >> 1
        cluster = cluster_ref[...]
        number = lax.broadcasted_iota(jnp.int32, (1, rows), 1).astype(jnp.float32)
        key = (cluster & -own).astype(jnp.float32) * spread + number
        column = jnp.broadcast_to(key, (8, rows)).T[:, :1]
        order = jnp.zeros((1, rows), jnp.float32)
        for low in range(0, rows, chunk):
            earlier = (column[low : low + chunk] < key).astype(jnp.float32)
            order = order + jnp.sum(earlier, axis=0, keepdims=True)
        order = order.astype(jnp.int32)
        order_ref[...] = order
        lane = lax.broadcasted_iota(jnp.int32, (1, 128), 1)
        starts = jnp.zeros((1, 128), jnp.int32)
        for at, step in ((ABOVE, 1), (HERE, 0), (BELOW, n_line - 1)):
            border = (2 * lax.rem(place + step, n_line) + 1) * own
            before = jnp.sum((cluster < border).astype(jnp.float32), axis=1, keepdims=True)
            start = ((before.astype(jnp.int32) + 1 - side) >> 1) - cap + half
            starts = jnp.where(lane == at, start, starts)
            if at == ABOVE:
                above = start
        starts_ref[...] = starts
        turned = (order >> 1) - above + 2 * half
        turned = jnp.where(turned >= 2 * half, turned - 2 * half, turned)
        turned = jnp.where(turned >= half, turned - half, turned)
        slot = jnp.where((order & 1) == side, turned, half + (order >> 1))
        for low in range(0, rows, chunk):
            hit = lax.broadcasted_iota(jnp.int32, (chunk, rows), 0) + low == slot
            found = product(hit.astype(jnp.float32).astype(jnp.bfloat16), rows_ref[...])
            out_ref, at = (kept_ref, low) if low < half else (given_ref, low - half)
            out_ref[at : at + chunk] = found.astype(jnp.bfloat16)

    return pl.pallas_call(
        kernel,
        grid_spec=pltpu.PrefetchScalarGridSpec(
            num_scalar_prefetch=1,
            grid=(1,),
            in_specs=[
                pl.BlockSpec((1, rows), lambda g, ids: (0, 0)),
                pl.BlockSpec((rows, width), lambda g, ids: (0, 0)),
            ],
            out_specs=[VMEM] * 4,
        ),
        out_shape=[
            jax.ShapeDtypeStruct((half, width), jnp.bfloat16),
            jax.ShapeDtypeStruct((half, width), jnp.bfloat16),
            jax.ShapeDtypeStruct((1, rows), jnp.int32),
            jax.ShapeDtypeStruct((1, 128), jnp.int32),
        ],
        compiler_params=PARAMS,
        cost_estimate=NO_COST,
        name="deal",
    )(ids, clusters, embeddings)


def between(starts_ref, has, wants, half):
    start = 0 if has is None else starts_ref[0, has]
    return lax.rem(starts_ref[0, wants] - start + 2 * half, half)


def turn(parts, starts, has, wants, first, count, split):
    half = sum(p.shape[0] for p in parts) if split else parts[0].shape[0]
    width = parts[0].shape[1] if split else sum(p.shape[1] for p in parts)

    def kernel(starts_ref, *refs):
        out_ref = refs[-1]
        hot = chosen_rows(between(starts_ref, has, wants, half), first, count, half)
        if split:
            near = refs[0].shape[0]
            total = product(hot[:, :near], refs[0][...]) + product(hot[:, near:], refs[1][...])
            out_ref[...] = total.astype(jnp.bfloat16)
        else:
            low = 0
            for ref in refs[:-1]:
                high = low + ref.shape[1]
                out_ref[:, low:high] = product(hot, ref[...]).astype(jnp.bfloat16)
                low = high

    return pl.pallas_call(
        kernel,
        in_specs=[SMEM] + [VMEM] * len(parts),
        out_specs=VMEM,
        out_shape=jax.ShapeDtypeStruct((count, width), jnp.bfloat16),
        compiler_params=PARAMS,
        cost_estimate=NO_COST,
        name="turn",
    )(starts, *parts)


def turn_down(kept, swapped, starts, near):
    half, width = kept.shape

    def kernel(starts_ref, kept_ref, swapped_ref, near_ref, far_ref):
        for n, (ref, has) in enumerate(((kept_ref, ABOVE), (swapped_ref, None))):
            hot = chosen_rows(between(starts_ref, has, BELOW, half), 0, half, half)
            rows = product(hot, ref[...]).astype(jnp.bfloat16)
            near_ref[:, n * width : (n + 1) * width] = rows[:near]
            far_ref[:, n * width : (n + 1) * width] = rows[near:]

    return pl.pallas_call(
        kernel,
        in_specs=[SMEM, VMEM, VMEM],
        out_specs=[VMEM, VMEM],
        out_shape=[
            jax.ShapeDtypeStruct((near, 2 * width), jnp.bfloat16),
            jax.ShapeDtypeStruct((half - near, 2 * width), jnp.bfloat16),
        ],
        compiler_params=PARAMS,
        cost_estimate=NO_COST,
        name="turn_down",
    )(starts, kept, swapped)


def take_share(ids, table, n_dp, late):
    count, depth = table.shape[0] // n_dp // (2 if late else 1), table.shape[1]

    def kernel(ids_ref, in_ref, out_ref):
        out_ref[...] = in_ref[...]

    return pl.pallas_call(
        kernel,
        grid_spec=pltpu.PrefetchScalarGridSpec(
            num_scalar_prefetch=1,
            grid=(1,),
            in_specs=[
                pl.BlockSpec(
                    (count, depth),
                    lambda g, ids: (2 * (ids[0] ^ (n_dp // 2)) + 1 if late else ids[0], 0),
                )
            ],
            out_specs=VMEM,
        ),
        out_shape=jax.ShapeDtypeStruct((count, depth), table.dtype),
        compiler_params=PARAMS,
        cost_estimate=NO_COST,
        name="take_share",
    )(ids, table)


def prepare(ids, starts, clusters, orders, kept, swapped, prior, table, cap):
    half, width = kept.shape
    n_dp, rows = clusters.shape
    own, feats = table.shape[0], table.shape[1] // n_dp

    def kernel(ids_ref, starts_ref, cluster_ref, order_ref, kept_ref, swapped_ref, prior_ref,
               table_ref, self_a, self_b, same_ref, across_ref, counts_ref, base_ref):
        for out_ref, ref, has in ((self_a, kept_ref, ABOVE), (self_b, swapped_ref, None)):
            hot = chosen_rows(between(starts_ref, has, HERE, half), 0, half, half)
            out_ref[...] = product(hot, ref[...]).astype(jnp.bfloat16)
        me = ids_ref[1]
        side, place = me & 1, me >> 1
        counts = jnp.zeros((1, own), jnp.float32)
        slot = lax.broadcasted_iota(jnp.int32, (cap, rows), 0)
        column = lax.broadcasted_iota(jnp.int32, (cap, own), 1).astype(jnp.float32)
        for m in range(n_dp):
            order, cluster = order_ref[m : m + 1, :], cluster_ref[m : m + 1, :]
            local = cluster - me * own
            local = jnp.where((local >= 0) & (local < own), local, own).astype(jnp.float32)
            earlier = (cluster < (2 * place + 1) * own).astype(jnp.float32)
            before = jnp.sum(earlier, axis=1, keepdims=True).astype(jnp.int32)
            for b, out_ref in enumerate((same_ref, across_ref)):
                which = side if b == 0 else 1 - side
                start = ((before + 1 - which) >> 1) - cap + half
                turned = (order >> 1) - start + 2 * half
                turned = jnp.where(turned >= 2 * half, turned - 2 * half, turned)
                turned = jnp.where(turned >= half, turned - half, turned)
                spot = jnp.where((order & 1) == which, turned - side * cap, rows)
                name = jnp.sum(jnp.where(slot == spot, local, 0.0), axis=1, keepdims=True)
                match = (column == name).astype(jnp.float32)
                out_ref[m * cap : (m + 1) * cap, :] = match.astype(jnp.bfloat16)
                counts = counts + jnp.sum(match, axis=0, keepdims=True)
        counts_ref[...] = counts
        base_ref[...] = table_ref[...].astype(jnp.float32).T * prior_ref[...]

    outs = [
        jax.ShapeDtypeStruct((half, width), jnp.bfloat16),
        jax.ShapeDtypeStruct((half, width), jnp.bfloat16),
        jax.ShapeDtypeStruct((n_dp * cap, own), jnp.bfloat16),
        jax.ShapeDtypeStruct((n_dp * cap, own), jnp.bfloat16),
        jax.ShapeDtypeStruct((1, own), jnp.float32),
        jax.ShapeDtypeStruct((feats, own), jnp.float32),
    ]
    return pl.pallas_call(
        kernel,
        grid_spec=pltpu.PrefetchScalarGridSpec(
            num_scalar_prefetch=2,
            grid=(1,),
            in_specs=[VMEM] * 5 + [pl.BlockSpec((own, feats), lambda g, ids, at: (0, ids[0]))],
            out_specs=[VMEM] * len(outs),
        ),
        out_shape=outs,
        compiler_params=PARAMS,
        cost_estimate=NO_COST,
        name="prepare",
    )(ids, starts, clusters, orders, kept, swapped, prior, table)


def collect(ids, windows, cap, n_dp):
    n_windows, per_dp = len(windows), len(windows) // n_dp
    wide = sum(part.shape[1] for part in windows[0])
    counts = [len(window) for window in windows]
    parts = [part for window in windows for part in window]

    def kernel(ids_ref, *refs):
        part_refs, out_refs = refs[: len(parts)], refs[len(parts) :]
        side, place = ids_ref[1] & 1, ids_ref[1] >> 1
        for m in range(n_dp):
            for e in range(per_dp):
                start = 0
                wanted = lax.rem(place - (ids_ref[0] ^ m) * per_dp - e + n_windows, n_windows)
                for n, count in enumerate(counts):

                    @pl.when(wanted == n)
                    def _(m=m, e=e, start=start, count=count):
                        low = e * wide
                        for ref in part_refs[start : start + count]:
                            high = low + ref.shape[1]
                            for b in (0, 1):
                                which = side if b == 0 else 1 - side
                                rows = pl.ds(pl.multiple_of(which * cap, cap), cap)
                                out_refs[2 * m + b][:, low:high] = ref[rows, :]
                            low = high

                    start += count

    outs = [jax.ShapeDtypeStruct((cap, per_dp * wide), jnp.bfloat16)] * (2 * n_dp)
    found = pl.pallas_call(
        kernel,
        in_specs=[SMEM] + [VMEM] * len(parts),
        out_specs=[VMEM] * len(outs),
        out_shape=outs,
        compiler_params=PARAMS,
        cost_estimate=NO_COST,
        name="collect",
    )(ids, *parts)
    return {(m, b): found[2 * m + b] for m in range(n_dp) for b in (0, 1)}


def update(ids, rows, matches, base, prior, counts, token, divide):
    n_rows, cap = len(rows), rows[0][2].shape[0]
    feats, own = base.shape
    width, n_blocks = feats // 2, 4
    block_rows = feats // n_blocks

    def kernel(ids_ref, *refs):
        row_refs, match_refs = refs[:n_rows], refs[n_rows : n_rows + 2]
        base_ref, prior_ref, counts_ref, token_ref, out_ref = refs[n_rows + 2 :]
        step = pl.program_id(0)
        for n in range(n_blocks):

            @pl.when(step == n)
            def _(n=n):
                held, match = [], []
                for (at, b, _), ref in zip(rows, row_refs):
                    low = ((2 * n // n_blocks) ^ b) * width + n * block_rows % width
                    held.append(ref[:, low : low + block_rows])
                    match.append(match_refs[b][at * cap : (at + 1) * cap])
                total = base_ref[...] + lax.dot_general(
                    jnp.concatenate(held, axis=0),
                    jnp.concatenate(match, axis=0),
                    (((0,), (0,)), ((), ())),
                    preferred_element_type=jnp.float32,
                )
                if divide:
                    nothing = token_ref[:1, :1].astype(jnp.float32)
                    total = total * (1.0 / (prior_ref[...] + counts_ref[...] + nothing))
                out_ref[...] = total

    each = n_blocks // 2
    block = pl.BlockSpec(
        (block_rows, own), lambda g, ids: ((g // each ^ (ids[1] & 1)) * each + g % each, 0)
    )
    return pl.pallas_call(
        kernel,
        grid_spec=pltpu.PrefetchScalarGridSpec(
            num_scalar_prefetch=1,
            grid=(n_blocks,),
            in_specs=[VMEM] * (n_rows + 2) + [block, VMEM, VMEM, VMEM],
            out_specs=block,
        ),
        out_shape=jax.ShapeDtypeStruct((feats, own), jnp.float32),
        compiler_params=PARAMS,
        cost_estimate=NO_COST,
        name="update",
    )(ids, *[value for _, _, value in rows], *matches, base, prior, counts, token)


def column_block(n_line, steps):
    def block(g, ids):
        side, place = ids[1] & 1, ids[1] >> 1
        step = steps[-1]
        for n, other in enumerate(steps[:-1]):
            step = jnp.where(g // 2 == n, other, step)
        return 2 * lax.rem(place - step + n_line, n_line) + (side ^ (g % 2))

    return block


def score_part(ids, tables, work, half, n_line, so_far=None):
    sizes = [table.shape[0] for table in tables]
    total, width = sum(sizes), tables[0].shape[1] // (2 * n_line)
    n_tables, n_blocks = len(tables), 2 * len(work)
    block = column_block(n_line, [step for step, _ in work])
    parts = [part for _, piece in work for part in piece]
    before = [] if so_far is None else [so_far]

    def kernel(ids_ref, *refs):
        table_refs, part_refs = refs[:n_tables], list(refs[n_tables : n_tables + len(parts)])
        before_refs = refs[n_tables + len(parts) : -5]
        out_ref, best_ref, piece, score, squares = refs[-5:]
        step = pl.program_id(0)

        @pl.when(step == 0)
        def _():
            score[...] = before_refs[0][...] if before_refs else jnp.zeros_like(score)
            squares[...] = jnp.zeros_like(squares)

        for at, (_, held) in enumerate(work):
            held_refs = [part_refs.pop(0) for _ in held]
            for n in (0, 1):

                @pl.when(step == 2 * at + n)
                def _(n=n, held_refs=held_refs):
                    if held_refs[0].shape[1] == width:
                        piece[...] = held_refs[n][...]
                    else:
                        low = 0
                        for ref in held_refs:
                            high = low + ref.shape[0]
                            piece[low:high] = ref[:, n * width : (n + 1) * width]
                            low = high
                        if low < half:
                            piece[low:] = jnp.zeros((half - low, width), piece.dtype)

        low = 0
        for ref, size in zip(table_refs, sizes):
            score[low : low + size] += lax.dot_general(
                ref[...], piece[...], (((1,), (1,)), ((), ())), preferred_element_type=jnp.float32
            )
            for lane in range(0, width, 128):
                entries = ref[:, lane : lane + 128].astype(jnp.float32)
                squares[low : low + size] += entries * entries
            low += size

        @pl.when(step == n_blocks - 1)
        def _():
            final = score[...] - 0.5 * jnp.sum(squares[...], axis=1, keepdims=True)
            out_ref[...] = final
            best_ref[...] = jnp.max(final, axis=0, keepdims=True)

    grid_spec = pltpu.PrefetchScalarGridSpec(
        num_scalar_prefetch=1,
        grid=(n_blocks,),
        in_specs=[
            pl.BlockSpec((size, width), lambda g, ids: (0, block(g, ids))) for size in sizes
        ]
        + [VMEM] * (len(parts) + len(before)),
        out_specs=[VMEM, VMEM],
        scratch_shapes=[
            pltpu.VMEM((half, width), jnp.bfloat16),
            pltpu.VMEM((total, half), jnp.float32),
            pltpu.VMEM((total, 128), jnp.float32),
        ],
    )
    return pl.pallas_call(
        kernel,
        grid_spec=grid_spec,
        out_shape=[
            jax.ShapeDtypeStruct((total, half), jnp.float32),
            jax.ShapeDtypeStruct((1, half), jnp.float32),
        ],
        compiler_params=PARAMS,
        cost_estimate=NO_COST,
        name="score_part",
    )(ids, *tables, *parts, *before)


def score_last(ids, starts, tables, last, scores, bests, order, near, n_line):
    count, width = last.shape[0], last.shape[1] // 2
    half, rows = scores[0].shape[1], order.shape[1]
    sizes = [table.shape[0] for table in tables]
    total, n_tables, n_scores = sum(sizes), len(tables), len(scores)
    block = column_block(n_line, [n_line // 2])
    low_row = near if near % 128 == 0 else 0

    def kernel(ids_ref, starts_ref, *refs):
        table_refs, last_ref = refs[:n_tables], refs[n_tables]
        score_refs = refs[n_tables + 1 : n_tables + 1 + n_scores]
        best_refs = refs[n_tables + 1 + n_scores : n_tables + 1 + 2 * n_scores]
        order_ref, out_ref, piece, sums = refs[n_tables + 1 + 2 * n_scores :]
        step = pl.program_id(0)
        if low_row < near:
            piece[: near - low_row] = jnp.zeros((near - low_row, width), piece.dtype)
        for n in (0, 1):

            @pl.when(step == n)
            def _(n=n):
                piece[near - low_row :] = last_ref[:, n * width : (n + 1) * width]

        low = 0
        for ref, size in zip(table_refs, sizes):
            part = lax.dot_general(
                ref[...], piece[...], (((1,), (1,)), ((), ())), preferred_element_type=jnp.float32
            )
            sums[low : low + size] = part + jnp.where(step == 0, 0.0, sums[low : low + size])
            low += size

        @pl.when(step == 1)
        def _():
            late, low = [], 0
            for ref in score_refs:
                high = low + ref.shape[0]
                score = sums[low:high] + ref[:, low_row:]
                late.append(jnp.max(score, axis=0, keepdims=True))
                low = high
            row = largest_of(late)
            if low_row:
                first = largest_of([ref[:, :low_row] for ref in best_refs])
                row = jnp.concatenate([first, row], axis=1)
            column = jnp.broadcast_to(row, (8, half)).T[:, :1]
            side = ids_ref[1] & 1
            order = order_ref[...]
            turned = (order >> 1) - starts_ref[0, HERE] + 2 * half
            turned = jnp.where(turned >= 2 * half, turned - 2 * half, turned)
            turned = jnp.where(turned >= half, turned - half, turned)
            ours = (order & 1) == side
            found = lax.broadcasted_iota(jnp.int32, (half, rows), 0) == turned
            best = jnp.sum(jnp.where(found, column, 0.0), axis=0, keepdims=True)
            out_ref[...] = jnp.where(ours, best, -jnp.inf)

    grid_spec = pltpu.PrefetchScalarGridSpec(
        num_scalar_prefetch=2,
        grid=(2,),
        in_specs=[
            pl.BlockSpec((size, width), lambda g, ids, at: (0, block(g, ids))) for size in sizes
        ]
        + [VMEM] * (2 + 2 * n_scores),
        out_specs=VMEM,
        scratch_shapes=[
            pltpu.VMEM((half - low_row, width), jnp.bfloat16),
            pltpu.VMEM((total, half - low_row), jnp.float32),
        ],
    )
    return pl.pallas_call(
        kernel,
        grid_spec=grid_spec,
        out_shape=jax.ShapeDtypeStruct((1, rows), jnp.float32),
        compiler_params=PARAMS,
        cost_estimate=NO_COST,
        name="score_last",
    )(ids, starts, *tables, last, *scores, *bests, order)


def on_device(embeddings, centroids, assignment, prior_counts):
    n_dp, n_cent = lax.axis_size("dp"), lax.axis_size("cent")
    rows, width = embeddings.shape
    own, depth = centroids.shape
    half, n_line = rows // 2, n_cent // 2
    per_dp = n_line // n_dp
    cap = rows // n_cent
    near = 2 * cap
    middle = n_line // 2
    me_dp, me = lax.axis_index("dp"), lax.axis_index("cent")
    side, place = me % 2, me // 2
    swap = [(j, j ^ 1) for j in range(n_cent)]

    def ring(shift):
        return [(j, (j + 2 * shift) % n_cent) for j in range(n_cent)]

    def send(value, pairs):
        return lax.ppermute(value, "cent", pairs)

    ids = jnp.stack([me_dp, me])
    kept, given, order, starts = deal(ids, assignment[None, :], embeddings, own, cap, n_line)

    steps = Steps()
    kept, given, assignment, order, centroids, ids, starts = steps.tie(
        kept, given, assignment, order, centroids, ids, starts
    )
    up_a, swapped = send(kept, ring(1)), send(given, swap)
    blocks = jnp.stack([assignment[None, :], order], axis=1)
    prior = prior_counts.astype(jnp.float32)[None, :]
    share = take_share(ids, centroids, n_dp, False)

    swapped, share, blocks, prior, order = steps.tie(swapped, share, blocks, prior, order)
    up_b, up_a = steps.tie(turn([swapped], starts, None, ABOVE, 0, half, False), up_a)
    up_b = send(up_b, ring(1))
    close, far = steps.tie(*turn_down(kept, swapped, starts, near))
    close, share = send(close, ring(-1)), send(steps.tie(share), swap)

    blocks, held_from = steps.tie(blocks), [0]
    bit = n_dp // 2
    while bit:
        pairs = [(d, d ^ bit) for d in range(n_dp)]
        blocks = jnp.concatenate([blocks, lax.ppermute(blocks, "dp", pairs)], axis=0)
        held_from = held_from + [m ^ bit for m in held_from]
        bit //= 2
        blocks = steps.tie(blocks)

    ids, centroids = steps.tie(ids, centroids)
    late_share = take_share(ids, centroids, n_dp, True)

    up_b, late_share = steps.tie(up_b, late_share)
    up = (up_a, up_b)
    pieces = {1: up}
    for step in range(2, middle):
        wide = send(turn(list(up), starts, HERE, ABOVE, 0, half, False), ring(1))
        up = (wide[:, :width], wide[:, width:])
        pieces[step] = up
    middle_near = steps.tie(turn(list(up), starts, HERE, ABOVE, 0, near, False))
    middle_near = send(middle_near, ring(1))
    share, late_share = steps.tie(share, late_share)

    others, bit = [share], n_dp // 2
    if n_dp == 4:
        pairs = [(d, d ^ bit) for d in range(n_dp)]
        others = [
            share,
            lax.ppermute(share[: share.shape[0] // 2], "dp", pairs),
            send(late_share, swap),
        ]
    else:
        while bit > 1:
            pairs = [(d, d ^ bit) for d in range(n_dp)]
            others = others + [lax.ppermute(p, "dp", pairs) for p in others]
            bit //= 2
    clusters, orders, centroids = steps.tie(blocks[:, 0], blocks[:, 1], centroids)
    self_a, self_b, same, across, counts, base = prepare(
        ids, starts, clusters, orders, kept, swapped, prior, centroids, cap
    )
    pieces[0] = (self_a, self_b)

    middle_near, close, pieces[0], same, across, counts, base = steps.tie(
        middle_near, close, pieces[0], same, across, counts, base
    )
    far = send(steps.tie(far), ring(-1))
    windows = dict(pieces)
    windows[middle], windows[n_line - 1] = (middle_near,), (close,)

    down = (close, far)
    downs = {n_line - 1: down}

    def deliver(value, m, b):
        pairs = [
            (d * n_cent + j, (d ^ m) * n_cent + (j ^ b)) for d in range(n_dp) for j in range(n_cent)
        ]
        return lax.ppermute(value, ("dp", "cent"), pairs)

    for step in range(2, middle):
        down = tuple(
            send(turn(list(down), starts, HERE, BELOW, first, count, True), ring(-1))
            for first, count in ((0, near), (near, half - near))
        )
        downs[n_line - step] = down
        windows[n_line - step] = (down[0],)
    first = [(2, 0), (0, 1), (1, 0)]
    second = [(m, 0) for m in range(3, n_dp)] + [(m, 1) for m in range(1, n_dp)]
    got = steps.tie(collect(ids, [windows[n] for n in range(n_line)], cap, n_dp))
    others = steps.tie(others)
    core_sent = steps.tie(jnp.concatenate(others, axis=0))
    core = lax.ppermute(core_sent, "dp", [(d, d ^ 1) for d in range(n_dp)])
    for key in first:
        got[key] = deliver(got[key], *key)

    core, pieces = steps.tie(core, pieces)
    tables = [centroids, core_sent, core]
    work = [(step, pieces[step]) for step in pieces] + [(middle, (middle_near,))]
    so_far, _ = score_part(ids, tables, work, half, n_line)
    so_far = steps.tie(so_far)
    got.update(zip(first, steps.tie(*[got[key] for key in first])))

    downs[n_line - 1] = (close, steps.tie(downs[n_line - 1][1]))
    middle_far = steps.tie(
        turn(list(downs[middle + 1]), starts, HERE, BELOW, near, half - near, True)
    )
    middle_far = send(middle_far, ring(-1))
    for key, value in zip(second, steps.tie(*[got[key] for key in second])):
        got[key] = deliver(value, *key)
    downs = steps.tie(downs)
    work = [(step, downs[step]) for step in downs]
    score, best = steps.tie(*score_part(ids, tables, work, half, n_line, so_far))

    def payloads(keys):
        return [(held_from.index(m), b, got[m, b]) for m, b in keys]

    matches = [same, across]
    if per_dp == 1:
        early = [(0, 0)] + first
        base = update(ids, payloads(early), matches, base, prior, counts, steps.token, False)
        base = steps.tie(base)

    middle_far = steps.tie(middle_far)
    best = score_last(
        ids, starts, tables, middle_far, [score], [best], order, near, n_line
    )[0]
    best = steps.tie(best)
    bit = 1
    while bit < n_line:
        pairs = [(j, j ^ (2 * bit)) for j in range(n_cent)]
        best = steps.tie(jnp.maximum(best, send(best, pairs)))
        bit *= 2
    opposite = send(best, swap)

    got = steps.tie(got)
    feats = 2 * per_dp * width
    if per_dp == 1:
        updated = update(
            ids, payloads(second), matches, base, prior, counts, steps.token, True
        )
    else:
        counts = counts + steps.token[0, 0].astype(jnp.float32)

        def summed(match, b):
            held = jnp.concatenate([got[m, b] for m in held_from], axis=0)
            total = lax.dot_general(
                held, match, (((0,), (0,)), ((), ())), preferred_element_type=jnp.float32
            )
            return total.reshape(per_dp, 2, width, own)

        from_same, from_across = summed(same, 0), summed(across, 1)
        mine = from_same[:, 0] + from_across[:, 1]
        theirs = from_same[:, 1] + from_across[:, 0]
        even = jnp.where(side == 0, mine, theirs)
        odd = jnp.where(side == 0, theirs, mine)
        sums = jnp.stack([even, odd], axis=1).reshape(base.shape)
        updated = (base + sums) / (prior + counts)
    return (jnp.maximum(best, opposite), updated)


def largest_of(values):
    largest = values[0]
    for value in values[1:]:
        largest = jnp.maximum(largest, value)
    return largest


def solution(mesh):
    placed = (P("dp", "cent"), P("cent", None), P("dp"), P("cent"))
    return jax.shard_map(
        on_device, mesh=mesh, in_specs=placed, out_specs=(P("dp"), P("dp", "cent")), check_vma=False
    )
```

```python
import jax
import jax.numpy as jnp
from jax import lax
from jax.experimental import pallas as pl
from jax.experimental.pallas import tpu as pltpu
from jax.sharding import PartitionSpec as P

VMEM = pl.BlockSpec(memory_space=pltpu.VMEM)
SMEM = pl.BlockSpec(memory_space=pltpu.SMEM)
NO_COST = pl.CostEstimate(flops=0, bytes_accessed=0, transcendentals=0)
PARAMS = pltpu.CompilerParams(vmem_limit_bytes=16 * 1024 * 1024)

ABOVE, HERE, BELOW = 0, 1, 2


class Steps:
    def __init__(self):
        self.token = jnp.zeros((8, 128), jnp.int32)

    def tie(self, *values):
        self.token, values = lax.optimization_barrier((self.token, values))
        return values[0] if len(values) == 1 else values


def chosen_rows(shift, first, count, half):
    at = lax.broadcasted_iota(jnp.int32, (count, half), 0) + (shift + first)
    at = jnp.where(at >= half, at - half, at)
    at = jnp.where(at >= half, at - half, at)
    hit = at == lax.broadcasted_iota(jnp.int32, (count, half), 1)
    return hit.astype(jnp.float32).astype(jnp.bfloat16)


def product(hot, rows):
    return jnp.dot(hot, rows, preferred_element_type=jnp.float32)


def between(starts_ref, has, wants, half):
    start = 0 if has is None else starts_ref[has]
    return lax.rem(starts_ref[wants] - start + 2 * half, half)


def turn(parts, starts, has, wants, first, count, split):
    half = sum(p.shape[0] for p in parts) if split else parts[0].shape[0]
    width = parts[0].shape[1] if split else sum(p.shape[1] for p in parts)

    def kernel(starts_ref, *refs):
        out_ref = refs[-1]
        hot = chosen_rows(between(starts_ref, has, wants, half), first, count, half)
        if split:
            near = refs[0].shape[0]
            total = product(hot[:, :near], refs[0][...]) + product(hot[:, near:], refs[1][...])
            out_ref[...] = total.astype(jnp.bfloat16)
        else:
            low = 0
            for ref in refs[:-1]:
                high = low + ref.shape[1]
                out_ref[:, low:high] = product(hot, ref[...]).astype(jnp.bfloat16)
                low = high

    return pl.pallas_call(
        kernel,
        in_specs=[SMEM] + [VMEM] * len(parts),
        out_specs=VMEM,
        out_shape=jax.ShapeDtypeStruct((count, width), jnp.bfloat16),
        compiler_params=PARAMS,
        cost_estimate=NO_COST,
        name="turn",
    )(starts, *parts)


def turn_down(kept, swapped, starts, near):
    half, width = kept.shape

    def kernel(starts_ref, kept_ref, swapped_ref, near_ref, far_ref):
        for n, (ref, has) in enumerate(((kept_ref, ABOVE), (swapped_ref, None))):
            hot = chosen_rows(between(starts_ref, has, BELOW, half), 0, half, half)
            rows = product(hot, ref[...]).astype(jnp.bfloat16)
            near_ref[:, n * width : (n + 1) * width] = rows[:near]
            far_ref[:, n * width : (n + 1) * width] = rows[near:]

    return pl.pallas_call(
        kernel,
        in_specs=[SMEM, VMEM, VMEM],
        out_specs=[VMEM, VMEM],
        out_shape=[
            jax.ShapeDtypeStruct((near, 2 * width), jnp.bfloat16),
            jax.ShapeDtypeStruct((half - near, 2 * width), jnp.bfloat16),
        ],
        compiler_params=PARAMS,
        cost_estimate=NO_COST,
        name="turn_down",
    )(starts, kept, swapped)


def take_share(ids, table, n_dp, late):
    count, depth = table.shape[0] // n_dp // (2 if late else 1), table.shape[1]

    def kernel(ids_ref, in_ref, out_ref):
        out_ref[...] = in_ref[...]

    return pl.pallas_call(
        kernel,
        grid_spec=pltpu.PrefetchScalarGridSpec(
            num_scalar_prefetch=1,
            grid=(1,),
            in_specs=[
                pl.BlockSpec(
                    (count, depth),
                    lambda g, ids: (2 * (ids[0] ^ (n_dp // 2)) + 1 if late else ids[0], 0),
                )
            ],
            out_specs=VMEM,
        ),
        out_shape=jax.ShapeDtypeStruct((count, depth), table.dtype),
        compiler_params=PARAMS,
        cost_estimate=NO_COST,
        name="take_share",
    )(ids, table)


def prepare(ids, starts, clusters, orders, kept, swapped, prior, table, cap):
    half, width = kept.shape
    n_dp, rows = clusters.shape
    own, feats = table.shape[0], table.shape[1] // n_dp

    def kernel(ids_ref, starts_ref, cluster_ref, order_ref, kept_ref, swapped_ref, prior_ref,
               table_ref, self_a, self_b, same_ref, across_ref, counts_ref, base_ref):
        for out_ref, ref, has in ((self_a, kept_ref, ABOVE), (self_b, swapped_ref, None)):
            hot = chosen_rows(between(starts_ref, has, HERE, half), 0, half, half)
            out_ref[...] = product(hot, ref[...]).astype(jnp.bfloat16)
        me = ids_ref[1]
        side, place = me & 1, me >> 1
        counts = jnp.zeros((1, own), jnp.float32)
        slot = lax.broadcasted_iota(jnp.int32, (cap, rows), 0)
        column = lax.broadcasted_iota(jnp.int32, (cap, own), 1).astype(jnp.float32)
        for m in range(n_dp):
            order, cluster = order_ref[m : m + 1, :], cluster_ref[m : m + 1, :]
            local = cluster - me * own
            local = jnp.where((local >= 0) & (local < own), local, own).astype(jnp.float32)
            earlier = (cluster < (2 * place + 1) * own).astype(jnp.float32)
            before = jnp.sum(earlier, axis=1, keepdims=True).astype(jnp.int32)
            for b, out_ref in enumerate((same_ref, across_ref)):
                which = side if b == 0 else 1 - side
                start = ((before + 1 - which) >> 1) - cap + half
                turned = (order >> 1) - start + 2 * half
                turned = jnp.where(turned >= 2 * half, turned - 2 * half, turned)
                turned = jnp.where(turned >= half, turned - half, turned)
                spot = jnp.where((order & 1) == which, turned - side * cap, rows)
                name = jnp.sum(jnp.where(slot == spot, local, 0.0), axis=1, keepdims=True)
                match = (column == name).astype(jnp.float32)
                out_ref[m * cap : (m + 1) * cap, :] = match.astype(jnp.bfloat16)
                counts = counts + jnp.sum(match, axis=0, keepdims=True)
        counts_ref[...] = counts
        base_ref[...] = table_ref[...].astype(jnp.float32).T * prior_ref[...]

    outs = [
        jax.ShapeDtypeStruct((half, width), jnp.bfloat16),
        jax.ShapeDtypeStruct((half, width), jnp.bfloat16),
        jax.ShapeDtypeStruct((n_dp * cap, own), jnp.bfloat16),
        jax.ShapeDtypeStruct((n_dp * cap, own), jnp.bfloat16),
        jax.ShapeDtypeStruct((1, own), jnp.float32),
        jax.ShapeDtypeStruct((feats, own), jnp.float32),
    ]
    return pl.pallas_call(
        kernel,
        grid_spec=pltpu.PrefetchScalarGridSpec(
            num_scalar_prefetch=2,
            grid=(1,),
            in_specs=[VMEM] * 5 + [pl.BlockSpec((own, feats), lambda g, ids, at: (0, ids[0]))],
            out_specs=[VMEM] * len(outs),
        ),
        out_shape=outs,
        compiler_params=PARAMS,
        cost_estimate=NO_COST,
        name="prepare",
    )(ids, starts, clusters, orders, kept, swapped, prior, table)


def collect(ids, windows, cap, n_dp):
    n_windows, per_dp = len(windows), len(windows) // n_dp
    wide = sum(part.shape[1] for part in windows[0])
    counts = [len(window) for window in windows]
    parts = [part for window in windows for part in window]

    def kernel(ids_ref, *refs):
        part_refs, out_refs = refs[: len(parts)], refs[len(parts) :]
        side, place = ids_ref[1] & 1, ids_ref[1] >> 1
        for m in range(n_dp):
            for e in range(per_dp):
                start = 0
                wanted = lax.rem(place - (ids_ref[0] ^ m) * per_dp - e + n_windows, n_windows)
                for n, count in enumerate(counts):

                    @pl.when(wanted == n)
                    def _(m=m, e=e, start=start, count=count):
                        low = e * wide
                        for ref in part_refs[start : start + count]:
                            high = low + ref.shape[1]
                            for b in (0, 1):
                                which = side if b == 0 else 1 - side
                                rows = pl.ds(pl.multiple_of(which * cap, cap), cap)
                                out_refs[2 * m + b][:, low:high] = ref[rows, :]
                            low = high

                    start += count

    outs = [jax.ShapeDtypeStruct((cap, per_dp * wide), jnp.bfloat16)] * (2 * n_dp)
    found = pl.pallas_call(
        kernel,
        in_specs=[SMEM] + [VMEM] * len(parts),
        out_specs=[VMEM] * len(outs),
        out_shape=outs,
        compiler_params=PARAMS,
        cost_estimate=NO_COST,
        name="collect",
    )(ids, *parts)
    return {(m, b): found[2 * m + b] for m in range(n_dp) for b in (0, 1)}


def update(ids, rows, matches, base, prior, counts, token, divide):
    n_rows, cap = len(rows), rows[0][2].shape[0]
    feats, own = base.shape
    width = feats // 2

    def kernel(ids_ref, *refs):
        row_refs, match_refs = refs[:n_rows], refs[n_rows : n_rows + 2]
        base_ref, prior_ref, counts_ref, token_ref, out_ref = refs[n_rows + 2 :]
        for side in (0, 1):

            @pl.when(ids_ref[1] & 1 == side)
            def _(side=side):
              for n in (0, 1):
                low = (n ^ side) * width
                held, match = [], []
                for (at, b, _), ref in zip(rows, row_refs):
                    part = n ^ b
                    held.append(ref[:, part * width : (part + 1) * width])
                    match.append(match_refs[b][at * cap : (at + 1) * cap])
                total = base_ref[low : low + width] + lax.dot_general(
                    jnp.concatenate(held, axis=0),
                    jnp.concatenate(match, axis=0),
                    (((0,), (0,)), ((), ())),
                    preferred_element_type=jnp.float32,
                )
                if divide:
                    nothing = token_ref[:1, :1].astype(jnp.float32)
                    total = total * (1.0 / (prior_ref[...] + counts_ref[...] + nothing))
                out_ref[low : low + width] = total

    block = pl.BlockSpec((feats, own), lambda g, ids: (0, 0))
    return pl.pallas_call(
        kernel,
        grid_spec=pltpu.PrefetchScalarGridSpec(
            num_scalar_prefetch=1,
            grid=(1,),
            in_specs=[VMEM] * (n_rows + 6),
            out_specs=block,
        ),
        out_shape=jax.ShapeDtypeStruct((feats, own), jnp.float32),
        compiler_params=PARAMS,
        cost_estimate=NO_COST,
        name="update",
    )(ids, *[value for _, _, value in rows], *matches, base, prior, counts, token)


def column_block(n_line, steps):
    def block(g, ids):
        side, place = ids[1] & 1, ids[1] >> 1
        step = steps[-1]
        for n, other in enumerate(steps[:-1]):
            step = jnp.where(g // 2 == n, other, step)
        return 2 * lax.rem(place - step + n_line, n_line) + (side ^ (g % 2))

    return block


def score_part(ids, tables, work, half, n_line, so_far=None):
    sizes = [table.shape[0] for table in tables]
    total, width = sum(sizes), tables[0].shape[1] // (2 * n_line)
    n_tables, n_blocks = len(tables), 2 * len(work)
    block = column_block(n_line, [step for step, _ in work])
    parts = [part for _, piece in work for part in piece]
    before = [] if so_far is None else [so_far]

    def kernel(ids_ref, *refs):
        table_refs, part_refs = refs[:n_tables], list(refs[n_tables : n_tables + len(parts)])
        before_refs = refs[n_tables + len(parts) : -5]
        out_ref, best_ref, piece, score, squares = refs[-5:]
        step = pl.program_id(0)

        @pl.when(step == 0)
        def _():
            score[...] = before_refs[0][...] if before_refs else jnp.zeros_like(score)
            squares[...] = jnp.zeros_like(squares)

        for at, (_, held) in enumerate(work):
            held_refs = [part_refs.pop(0) for _ in held]
            for n in (0, 1):

                @pl.when(step == 2 * at + n)
                def _(n=n, held_refs=held_refs):
                    if held_refs[0].shape[1] == width:
                        piece[...] = held_refs[n][...]
                    else:
                        low = 0
                        for ref in held_refs:
                            high = low + ref.shape[0]
                            piece[low:high] = ref[:, n * width : (n + 1) * width]
                            low = high
                        if low < half:
                            piece[low:] = jnp.zeros((half - low, width), piece.dtype)

        low = 0
        for ref, size in zip(table_refs, sizes):
            score[low : low + size] += lax.dot_general(
                ref[...], piece[...], (((1,), (1,)), ((), ())), preferred_element_type=jnp.float32
            )
            for lane in range(0, width, 128):
                entries = ref[:, lane : lane + 128].astype(jnp.float32)
                squares[low : low + size] += entries * entries
            low += size

        @pl.when(step == n_blocks - 1)
        def _():
            final = score[...] - 0.5 * jnp.sum(squares[...], axis=1, keepdims=True)
            out_ref[...] = final
            best_ref[...] = jnp.max(final, axis=0, keepdims=True)

    grid_spec = pltpu.PrefetchScalarGridSpec(
        num_scalar_prefetch=1,
        grid=(n_blocks,),
        in_specs=[
            pl.BlockSpec((size, width), lambda g, ids: (0, block(g, ids))) for size in sizes
        ]
        + [VMEM] * (len(parts) + len(before)),
        out_specs=[VMEM, VMEM],
        scratch_shapes=[
            pltpu.VMEM((half, width), jnp.bfloat16),
            pltpu.VMEM((total, half), jnp.float32),
            pltpu.VMEM((total, 128), jnp.float32),
        ],
    )
    return pl.pallas_call(
        kernel,
        grid_spec=grid_spec,
        out_shape=[
            jax.ShapeDtypeStruct((total, half), jnp.float32),
            jax.ShapeDtypeStruct((1, half), jnp.float32),
        ],
        compiler_params=PARAMS,
        cost_estimate=NO_COST,
        name="score_part",
    )(ids, *tables, *parts, *before)


def score_last(ids, starts, tables, last, scores, bests, order, near, n_line):
    count, width = last.shape[0], last.shape[1] // 2
    half, rows = scores[0].shape[1], order.shape[1]
    sizes = [table.shape[0] for table in tables]
    total, n_tables, n_scores = sum(sizes), len(tables), len(scores)
    block = column_block(n_line, [n_line // 2])
    low_row = near if near % 128 == 0 else 0

    def kernel(ids_ref, starts_ref, *refs):
        table_refs, last_ref = refs[:n_tables], refs[n_tables]
        score_refs = refs[n_tables + 1 : n_tables + 1 + n_scores]
        best_refs = refs[n_tables + 1 + n_scores : n_tables + 1 + 2 * n_scores]
        order_ref, out_ref, piece, sums = refs[n_tables + 1 + 2 * n_scores :]
        if low_row < near:
            piece[: near - low_row] = jnp.zeros((near - low_row, 2 * width), piece.dtype)
        for side in (0, 1):

            @pl.when(ids_ref[1] & 1 == side)
            def _(side=side):
                for n in (0, 1):
                    low = (side ^ n) * width
                    part = last_ref[:, n * width : (n + 1) * width]
                    piece[near - low_row :, low : low + width] = part

        low = 0
        for ref, size in zip(table_refs, sizes):
            sums[low : low + size] = lax.dot_general(
                ref[...], piece[...], (((1,), (1,)), ((), ())), preferred_element_type=jnp.float32
            )
            low += size

        late, low = [], 0
        for ref in score_refs:
            high = low + ref.shape[0]
            score = sums[low:high] + ref[:, low_row:]
            late.append(jnp.max(score, axis=0, keepdims=True))
            low = high
        row = largest_of(late)
        if low_row:
            first = largest_of([ref[:, :low_row] for ref in best_refs])
            row = jnp.concatenate([first, row], axis=1)
        column = jnp.broadcast_to(row, (8, half)).T[:, :1]
        side = ids_ref[1] & 1
        order = order_ref[...]
        turned = (order >> 1) - starts_ref[HERE] + 2 * half
        turned = jnp.where(turned >= 2 * half, turned - 2 * half, turned)
        turned = jnp.where(turned >= half, turned - half, turned)
        ours = (order & 1) == side
        found = lax.broadcasted_iota(jnp.int32, (half, rows), 0) == turned
        best = jnp.sum(jnp.where(found, column, 0.0), axis=0, keepdims=True)
        out_ref[...] = jnp.where(ours, best, -jnp.inf)

    grid_spec = pltpu.PrefetchScalarGridSpec(
        num_scalar_prefetch=2,
        grid=(1,),
        in_specs=[
            pl.BlockSpec((size, 2 * width), lambda g, ids, at: (0, block(g, ids) // 2))
            for size in sizes
        ]
        + [VMEM] * (2 + 2 * n_scores),
        out_specs=VMEM,
        scratch_shapes=[
            pltpu.VMEM((half - low_row, 2 * width), jnp.bfloat16),
            pltpu.VMEM((total, half - low_row), jnp.float32),
        ],
    )
    return pl.pallas_call(
        kernel,
        grid_spec=grid_spec,
        out_shape=jax.ShapeDtypeStruct((1, rows), jnp.float32),
        compiler_params=PARAMS,
        cost_estimate=NO_COST,
        name="score_last",
    )(ids, starts, *tables, last, *scores, *bests, order)


def on_device(embeddings, centroids, assignment, prior_counts):
    n_dp, n_cent = lax.axis_size("dp"), lax.axis_size("cent")
    rows, width = embeddings.shape
    own, depth = centroids.shape
    half, n_line = rows // 2, n_cent // 2
    per_dp = n_line // n_dp
    cap = rows // n_cent
    near = 2 * cap
    middle = n_line // 2
    me_dp, me = lax.axis_index("dp"), lax.axis_index("cent")
    side, place = me % 2, me // 2
    swap = [(j, j ^ 1) for j in range(n_cent)]

    def ring(shift):
        return [(j, (j + 2 * shift) % n_cent) for j in range(n_cent)]

    def send(value, pairs):
        return lax.ppermute(value, "cent", pairs)

    ids = jnp.stack([me_dp, me])
    owner_of = assignment // own
    key = owner_of * rows + jnp.arange(rows, dtype=jnp.int32)
    order = jnp.sum(key[None, :] < key[:, None], axis=1, dtype=jnp.int32)
    parity, turn_no = order % 2, order // 2
    layers = (place + jnp.array([1, 0, n_line - 1], jnp.int32)) % n_line
    before = jnp.sum(owner_of[None, :] <= 2 * layers[:, None], axis=1, dtype=jnp.int32)
    starts = (before + 1 - side) // 2 - cap + half
    with jax.named_scope("deal_rows"):
        slot = jnp.where(parity == side, (turn_no - starts[ABOVE] + 2 * half) % half, half + turn_no)
        deal = jnp.arange(rows, dtype=jnp.int32)[:, None] == slot[None, :]
        dealt = lax.dot_general(
            deal.astype(jnp.bfloat16),
            embeddings,
            (((1,), (0,)), ((), ())),
            preferred_element_type=jnp.float32,
        ).astype(jnp.bfloat16)

    steps = Steps()
    kept, given, assignment, order, centroids, ids, starts = steps.tie(
        dealt[:half], dealt[half:], assignment, order, centroids, ids, starts
    )
    up_a, swapped = send(kept, ring(1)), send(given, swap)
    blocks = jnp.stack([assignment, order])[None]
    prior = prior_counts.astype(jnp.float32)[None, :]
    order = order[None, :]
    share = take_share(ids, centroids, n_dp, False)

    swapped, share, blocks, prior, order = steps.tie(swapped, share, blocks, prior, order)
    up_b, up_a = steps.tie(turn([swapped], starts, None, ABOVE, 0, half, False), up_a)
    up_b = send(up_b, ring(1))
    close, far = steps.tie(*turn_down(kept, swapped, starts, near))
    close, share = send(close, ring(-1)), send(steps.tie(share), swap)

    blocks, held_from = steps.tie(blocks), [0]
    bit = n_dp // 2
    while bit:
        pairs = [(d, d ^ bit) for d in range(n_dp)]
        blocks = jnp.concatenate([blocks, lax.ppermute(blocks, "dp", pairs)], axis=0)
        held_from = held_from + [m ^ bit for m in held_from]
        bit //= 2
        blocks = steps.tie(blocks)

    ids, centroids = steps.tie(ids, centroids)
    late_share = take_share(ids, centroids, n_dp, True)

    up_b, late_share = steps.tie(up_b, late_share)
    up = (up_a, up_b)
    pieces = {1: up}
    for step in range(2, middle):
        wide = send(turn(list(up), starts, HERE, ABOVE, 0, half, False), ring(1))
        up = (wide[:, :width], wide[:, width:])
        pieces[step] = up
    middle_near = steps.tie(turn(list(up), starts, HERE, ABOVE, 0, near, False))
    middle_near = send(middle_near, ring(1))
    share, late_share = steps.tie(share, late_share)

    others, bit = [share], n_dp // 2
    if n_dp == 4:
        pairs = [(d, d ^ bit) for d in range(n_dp)]
        others = [
            share,
            lax.ppermute(share[: share.shape[0] // 2], "dp", pairs),
            send(late_share, swap),
        ]
    else:
        while bit > 1:
            pairs = [(d, d ^ bit) for d in range(n_dp)]
            others = others + [lax.ppermute(p, "dp", pairs) for p in others]
            bit //= 2
    clusters, orders, centroids = steps.tie(blocks[:, 0], blocks[:, 1], centroids)
    self_a, self_b, same, across, counts, base = prepare(
        ids, starts, clusters, orders, kept, swapped, prior, centroids, cap
    )
    pieces[0] = (self_a, self_b)

    middle_near, close, pieces[0], same, across, counts, base = steps.tie(
        middle_near, close, pieces[0], same, across, counts, base
    )
    far = send(steps.tie(far), ring(-1))
    windows = dict(pieces)
    windows[middle], windows[n_line - 1] = (middle_near,), (close,)

    down = (close, far)
    downs = {n_line - 1: down}

    def deliver(value, m, b):
        pairs = [
            (d * n_cent + j, (d ^ m) * n_cent + (j ^ b)) for d in range(n_dp) for j in range(n_cent)
        ]
        return lax.ppermute(value, ("dp", "cent"), pairs)

    for step in range(2, middle):
        down = tuple(
            send(turn(list(down), starts, HERE, BELOW, first, count, True), ring(-1))
            for first, count in ((0, near), (near, half - near))
        )
        downs[n_line - step] = down
        windows[n_line - step] = (down[0],)
    first = [(2, 0), (0, 1), (1, 0)]
    second = [(m, 0) for m in range(3, n_dp)] + [(m, 1) for m in range(1, n_dp)]
    others = steps.tie(others)
    core_sent = steps.tie(jnp.concatenate(others, axis=0))
    core = lax.ppermute(core_sent, "dp", [(d, d ^ 1) for d in range(n_dp)])
    middle_near, close = steps.tie(middle_near, close)
    windows[middle], windows[n_line - 1] = (middle_near,), (close,)
    got = steps.tie(collect(ids, [windows[n] for n in range(n_line)], cap, n_dp))
    for key in first:
        got[key] = deliver(got[key], *key)

    core, pieces = steps.tie(core, pieces)
    tables = [centroids, core_sent, core]
    work = [(step, pieces[step]) for step in pieces] + [(middle, (middle_near,))]
    so_far, _ = score_part(ids, tables, work, half, n_line)
    so_far = steps.tie(so_far)
    got.update(zip(first, steps.tie(*[got[key] for key in first])))

    downs[n_line - 1] = (close, steps.tie(downs[n_line - 1][1]))
    middle_far = steps.tie(
        turn(list(downs[middle + 1]), starts, HERE, BELOW, near, half - near, True)
    )
    middle_far = send(middle_far, ring(-1))
    for key, value in zip(second, steps.tie(*[got[key] for key in second])):
        got[key] = deliver(value, *key)
    downs = steps.tie(downs)
    work = [(step, downs[step]) for step in downs]
    score, best = steps.tie(*score_part(ids, tables, work, half, n_line, so_far))

    def payloads(keys):
        return [(held_from.index(m), b, got[m, b]) for m, b in keys]

    matches = [same, across]
    if per_dp == 1:
        early = [(0, 0)] + first
        base = update(ids, payloads(early), matches, base, prior, counts, steps.token, False)
        base = steps.tie(base)

    middle_far = steps.tie(middle_far)
    best = score_last(
        ids, starts, tables, middle_far, [score], [best], order, near, n_line
    )[0]
    best = steps.tie(best)
    bit = 1
    while bit < n_line:
        pairs = [(j, j ^ (2 * bit)) for j in range(n_cent)]
        best = steps.tie(jnp.maximum(best, send(best, pairs)))
        bit *= 2
    opposite = send(best, swap)

    got = steps.tie(got)
    feats = 2 * per_dp * width
    if per_dp == 1:
        updated = update(
            ids, payloads(second), matches, base, prior, counts, steps.token, True
        )
    else:
        counts = counts + steps.token[0, 0].astype(jnp.float32)

        def summed(match, b):
            held = jnp.concatenate([got[m, b] for m in held_from], axis=0)
            total = lax.dot_general(
                held, match, (((0,), (0,)), ((), ())), preferred_element_type=jnp.float32
            )
            return total.reshape(per_dp, 2, width, own)

        from_same, from_across = summed(same, 0), summed(across, 1)
        mine = from_same[:, 0] + from_across[:, 1]
        theirs = from_same[:, 1] + from_across[:, 0]
        even = jnp.where(side == 0, mine, theirs)
        odd = jnp.where(side == 0, theirs, mine)
        sums = jnp.stack([even, odd], axis=1).reshape(base.shape)
        updated = (base + sums) / (prior + counts)
    return (jnp.maximum(best, opposite), updated)


def largest_of(values):
    largest = values[0]
    for value in values[1:]:
        largest = jnp.maximum(largest, value)
    return largest


def solution(mesh):
    placed = (P("dp", "cent"), P("cent", None), P("dp"), P("cent"))
    return jax.shard_map(
        on_device, mesh=mesh, in_specs=placed, out_specs=(P("dp"), P("dp", "cent")), check_vma=False
    )
```
